32 devices in a mesh: section: 8 (over z, x), tensor: 4 (over y, core).
Axes of the slice: x: 2, y: 2, z: 4, core: 2. Of those that a mesh axis runs over, the one named last changes fastest.
Arguments:
- old_query: bfloat16 [8, 4096, 4096], P('section', 'tensor'), may hold values from -0.09375 to 0.09375
- old_key: bfloat16 [8, 4096, 1024], P('section', 'tensor'), may hold values from -0.09375 to 0.09375
- old_value: bfloat16 [8, 4096, 1024], P('section', 'tensor'), may hold values from -0.09375 to 0.09375
- depth_mix: float32 [8], replicated, may hold values from -2 to 2
- width_query: bfloat16 [8192, 4096], P('section', 'tensor'), may hold values from -0.09375 to 0.09375
- width_kv: bfloat16 [1024, 1024], P('section', 'tensor'), may hold values from -0.1875 to 0.1875
- width_stream: bfloat16 [8192, 4096], P('tensor', 'section'), may hold values from -0.0625 to 0.0625
- hidden: bfloat16 [2048, 8192], P('section', 'tensor'), may hold values from -8 to 8
Outputs:
- grown_query: bfloat16 [8192, 8192], P('tensor', 'section')
- grown_key: bfloat16 [8192, 1024], P('tensor', 'section')
- grown_value: bfloat16 [8192, 1024], P('tensor', 'section')
- attended: bfloat16 [2048, 8192], P('tensor', 'section')
The draws below stay inside these ranges and needn't reach their ends.
All inputs are finite; a program needn't handle non-finite values.
Results may differ from the reference program's by a relative error of at most 0.034.
Values may be sent and summed in bfloat16 or wider, within the bound.
A program may use at most 128 MiB of HBM per device.

```python
import math
import jax
import jax.numpy as jnp
from jax import lax

D1 = 4096
D2 = 8192
HEADS = 64
HD = 128
KVH = 8
KVW = 1024
OLD = 8
SEQ_LEN = 2048


def draw_hidden(key, part):
    key = jax.random.fold_in(key, 11)
    base_key = jax.random.fold_in(key, 0)
    return jnp.clip(jax.random.normal(base_key, (SEQ_LEN, D2), jnp.float32), -4.0, 4.0).astype(jnp.bfloat16)


def level_of(key, extent, shards, least, top_value):
    def one(dim, blocks):
        steps = jax.random.uniform(jax.random.fold_in(jax.random.fold_in(key, 6), dim), (blocks,), jnp.float32, least / len(shards), top_value / len(shards))
        return jnp.repeat(jnp.exp(steps), extent[dim] // blocks).reshape((-1,) + (1,) * (len(extent) - dim - 1))

    factor_of = one(*shards[0])
    for cut in shards[1:]:
        factor_of = factor_of * one(*cut)
    return factor_of


def bell_draw(own_key, shape, deviation, limit, cuts=(), held_as=jnp.bfloat16):
    factor_of = level_of(own_key, shape, cuts, -0.22, 0.18) if cuts else 1.0
    array = jax.random.normal(own_key, shape, jnp.float32) * deviation * factor_of
    return jnp.minimum(jnp.maximum(array, -limit), limit).astype(held_as)


def setup_inputs(seed: int = 0) -> dict:
    key_of = jax.random.split(jax.random.key(seed), 9)
    old_query = bell_draw(key_of[0], (OLD, D1, D1), D1 ** -0.5, 0.09375, ((0, 8), (1, 4)))
    old_key = bell_draw(key_of[1], (OLD, D1, KVW), D1 ** -0.5, 0.09375, ((0, 8), (1, 4)))
    old_value = bell_draw(key_of[2], (OLD, D1, KVW), D1 ** -0.5, 0.09375, ((0, 8), (1, 4)))
    depth_mix = bell_draw(key_of[3], (OLD,), OLD ** -0.5, 2.0, (), jnp.float32)
    width_query = bell_draw(key_of[4], (D2, D1), D1 ** -0.5, 0.09375, ((0, 8), (1, 4)))
    width_kv = bell_draw(key_of[5], (KVW, KVW), KVW ** -0.5, 0.1875, ((0, 8), (1, 4)))
    width_stream = bell_draw(key_of[6], (D2, D1), D2 ** -0.5, 0.0625, ((0, 4), (1, 8)))
    hidden = draw_hidden(jax.random.fold_in(key_of[8], 71), 0)
    return dict(old_query=old_query, old_key=old_key, old_value=old_value, depth_mix=depth_mix, width_query=width_query, width_kv=width_kv, width_stream=width_stream, hidden=hidden)


def mix_layers(depth_mix, stacked):

    def add_layer(layer_index, running):
        return running + depth_mix[layer_index] * stacked[layer_index].astype(jnp.float32)
    initial = jnp.zeros(stacked.shape[1:], jnp.float32)
    return lax.fori_loop(0, stacked.shape[0], add_layer, initial).astype(jnp.bfloat16)

def contract_last(left_side, right_side):
    return lax.dot_general(left_side.astype(jnp.float32), right_side.astype(jnp.float32), (((1,), (1,)), ((), ())), preferred_element_type=jnp.float32)

def product(left_side, right_side):
    return jnp.dot(left_side.astype(jnp.float32), right_side.astype(jnp.float32), preferred_element_type=jnp.float32)

def reference(old_query, old_key, old_value, depth_mix, width_query, width_kv, width_stream, hidden):
    mixed_query = mix_layers(depth_mix, old_query)
    mixed_key = mix_layers(depth_mix, old_key)
    mixed_value = mix_layers(depth_mix, old_value)
    expanded_query = contract_last(mixed_query, width_query).astype(jnp.bfloat16)
    expanded_key = contract_last(mixed_key, width_kv).astype(jnp.bfloat16)
    expanded_value = contract_last(mixed_value, width_kv).astype(jnp.bfloat16)
    grown_query = product(width_stream, expanded_query).astype(jnp.bfloat16)
    grown_key = product(width_stream, expanded_key).astype(jnp.bfloat16)
    grown_value = product(width_stream, expanded_value).astype(jnp.bfloat16)
    joined = jnp.concatenate([grown_query, grown_key, grown_value], axis=1)
    projections = product(hidden, joined)
    queries = projections[:, :D2].astype(jnp.bfloat16)
    key_rows = projections[:, D2:D2 + KVW].astype(jnp.bfloat16)
    value_rows = projections[:, D2 + KVW:].astype(jnp.bfloat16)
    score_scale = 1.0 / math.sqrt(HD)
    positions = jnp.arange(SEQ_LEN, dtype=jnp.int32)
    causal = positions[None, :] <= positions[:, None]
    query_heads = queries.reshape(SEQ_LEN, HEADS, HD).transpose(1, 0, 2)
    key_heads = key_rows.reshape(SEQ_LEN, KVH, HD).transpose(1, 0, 2)
    value_heads = value_rows.reshape(SEQ_LEN, KVH, HD).transpose(1, 0, 2)

    def one_head(head_index):
        head_query = query_heads[head_index]
        head_key = key_heads[head_index % KVH]
        head_value = value_heads[head_index % KVH]
        scores = lax.dot_general(head_query, head_key, (((1,), (1,)), ((), ())), preferred_element_type=jnp.float32) * score_scale
        scores = jnp.where(causal, scores, -jnp.inf)
        row_max = lax.optimization_barrier(jnp.max(scores, axis=1, keepdims=True))
        weights = jnp.exp(scores - row_max)
        denominator = lax.optimization_barrier(jnp.sum(weights, axis=1, keepdims=True))
        probs = weights.astype(jnp.bfloat16)
        output = jnp.dot(probs, head_value, preferred_element_type=jnp.float32) / denominator
        return output.astype(jnp.bfloat16)
    heads_out = lax.map(one_head, jnp.arange(HEADS, dtype=jnp.int32))
    attended = heads_out.transpose(1, 0, 2).reshape(SEQ_LEN, D2)
    return (grown_query, grown_key, grown_value, attended)
```

```python
import functools
import math

import jax
import jax.numpy as jnp
from jax import lax
from jax.experimental import pallas as pl
from jax.experimental.pallas import tpu as pltpu
from jax.sharding import PartitionSpec as P

HD = 128
KVH = 8
MIB = 1024 * 1024
ANY = pl.BlockSpec(memory_space=pl.ANY)


def contract_last(left_side, right_side):
    return lax.dot_general(
        left_side, right_side, (((1,), (1,)), ((), ())), preferred_element_type=jnp.float32
    )


def remote(src, dst, send, recv, axis, index):
    return pltpu.make_async_remote_copy(
        src_ref=src,
        dst_ref=dst,
        send_sem=send,
        recv_sem=recv,
        device_id={axis: index},
        device_id_type=pl.DeviceIdType.MESH,
    )


class Place:
    def __init__(self, sections):
        self.count = sections // 2
        self.section = lax.axis_index("section")
        self.tensor = lax.axis_index("tensor")
        self.z = self.section // 2
        self.x = self.section % 2
        self.y = self.tensor // 2
        self.core = self.tensor % 2
        self.other_x = self.z * 2 + 1 - self.x
        self.other_y = (1 - self.y) * 2 + self.core
        self.other_core = self.y * 2 + 1 - self.core


class SectionGather:
    def __init__(self, place, own, view, sems, local_sem=None, on_block=None, wide=False):
        self.p = place
        self.own = view(place.section) if own is None else own
        self.view = view
        self.sems = sems
        self.local = None
        if local_sem is not None:
            self.local = pltpu.make_async_copy(self.own, view(place.section), local_sem)
        self.on_block = on_block
        self.wide = wide

    def copy(self, kind, origin, src):
        p = self.p
        target = (p.section + 2, p.section - 2, p.other_x)[kind - 1]
        return remote(
            src,
            self.view(origin),
            self.sems.at[kind, origin],
            self.sems.at[0, origin],
            "section",
            target,
        )

    def start_z(self):
        p = self.p

        @pl.when(p.z < p.count - 1)
        def _():
            self.copy(1, p.section, self.own).start()

        @pl.when(p.z > 0)
        def _():
            self.copy(2, p.section, self.own).start()

        if self.local is not None:
            self.local.start()

    def start_x(self):
        self.copy(3, self.p.section, self.own).start()

    def start(self):
        if self.wide:
            self.start_x()
            self.start_z()
        else:
            self.start_z()
            self.start_x()

    def arrived(self, origin):
        self.copy(3, origin, self.view(origin)).wait_recv()

    def cross(self):
        p = self.p
        if self.wide:
            origin = p.other_x
            block = self.view(origin)
            self.arrived(origin)

            @pl.when(p.z < p.count - 1)
            def _():
                self.copy(1, origin, block).start()

            @pl.when(p.z > 0)
            def _():
                self.copy(2, origin, block).start()

    def step(self, hop):
        p = self.p

        def take(origin, kind, more):
            block = self.view(origin)
            self.arrived(origin)

            @pl.when(more)
            def _():
                self.copy(kind, origin, block).start()

            if not self.wide:
                self.copy(3, origin, block).start()
            if self.on_block is not None:
                self.on_block(origin)

        columns = (p.section, p.other_x) if self.wide else (p.section,)

        @pl.when(p.z - hop >= 0)
        def _():
            for column in columns:
                take(column - 2 * hop, 1, p.z < p.count - 1)

        @pl.when(p.z + hop < p.count)
        def _():
            for column in columns:
                take(column + 2 * hop, 2, p.z > 0)

    def finish(self):
        p = self.p
        if self.local is not None:
            self.local.wait()
        if not self.wide:
            for other_z in range(p.count):
                across = other_z * 2 + 1 - p.x
                self.arrived(across)
                if self.on_block is not None:
                    self.on_block(across)
        for other_z in range(p.count):
            for column in (p.x, 1 - p.x) if self.wide else (p.x,):
                origin = other_z * 2 + column
                block = self.view(origin)

                @pl.when((other_z <= p.z) & (p.z < p.count - 1))
                def _():
                    self.copy(1, origin, block).wait_send()

                @pl.when((other_z >= p.z) & (p.z > 0))
                def _():
                    self.copy(2, origin, block).wait_send()

            if not self.wide:
                self.copy(3, origin, block).wait_send()
        if self.wide:
            self.copy(3, p.section, self.own).wait_send()


class TensorGather:
    def __init__(self, place, own, view, sems, local_sem):
        p = place
        mine, far = p.tensor, p.other_y
        self.local = pltpu.make_async_copy(own, view(mine), local_sem)
        self.to_y = remote(own, view(mine), sems.at[0], sems.at[1], "tensor", p.other_y)
        self.to_core = remote(own, view(mine), sems.at[2], sems.at[3], "tensor", p.other_core)
        self.far_to_core = remote(
            view(far), view(far), sems.at[4], sems.at[5], "tensor", p.other_core
        )

    def start(self):
        self.to_y.start()
        self.to_core.start()
        self.local.start()

    def forward(self):
        self.to_y.wait_recv()
        self.far_to_core.start()

    def finish(self):
        self.local.wait()
        self.to_y.wait_send()
        self.to_core.wait()
        self.far_to_core.wait()


PARTS = 2


def mix_kernel(
    sections,
    depth_mix,
    old_query,
    old_key,
    old_value,
    width_query,
    width_kv,
    width_stream,
    mixed_query,
    mixed_key,
    mixed_value,
    query_width,
    kv_width,
    fragment,
    held,
    peer,
    sums,
    up,
    down,
    mine,
    load_sems,
    pair_sems,
    ring_sems,
    mixed_sems,
    stream_sems,
    width_sems,
    local_sems,
):
    p = Place(sections)
    count = p.count
    rows = held.shape[1]
    part_rows = rows // PARTS
    q_cols = old_query.shape[1] // sections
    k_cols = old_key.shape[1] // sections
    fields = (
        (old_query, 0, q_cols),
        (old_key, q_cols, k_cols),
        (old_value, q_cols + k_cols, k_cols),
    )
    factor = depth_mix[p.section]
    peer_factor = depth_mix[p.other_x]

    def pair_copies(far):
        for i, (ref, first, width) in enumerate(fields):
            start = pl.multiple_of((far * 2 + 1 - p.x) * width, 128)
            yield remote(
                ref.at[:, pl.ds(start, width)],
                peer.at[far, :, pl.ds(first, width)],
                pair_sems.at[0, far, i],
                pair_sems.at[1, far, i],
                "section",
                p.other_x,
            )

    def at_distance(distance, act):
        @pl.when(p.z + distance < count)
        def _():
            act(p.z + distance)

        if distance:

            @pl.when(p.z - distance >= 0)
            def _():
                act(p.z - distance)

    def send_pair(far):
        for one in pair_copies(far):
            one.start()

    def pair_arrived(far):
        for one in pair_copies(far):
            one.wait_recv()

    at_distance(count - 1, send_pair)

    loads = []
    for far in range(count):
        for i, (ref, first, width) in enumerate(fields):
            start = pl.multiple_of((far * 2 + p.x) * width, 128)
            load = pltpu.make_async_copy(
                ref.at[:, pl.ds(start, width)],
                held.at[far, :, pl.ds(first, width)],
                load_sems.at[3 * far + i],
            )
            load.start()
            loads.append(load)

    stream_rows, stream_cols = width_stream.shape
    wide_rows = stream_rows // 4

    def stream_gather(index, window, wide):
        return SectionGather(
            p,
            width_stream.at[window],
            lambda s: fragment.at[
                window, pl.ds(pl.multiple_of(s * stream_cols, 128), stream_cols)
            ],
            stream_sems.at[index],
            local_sems.at[index],
            wide=wide,
        )

    wide_stream = stream_gather(0, pl.ds(0, wide_rows), True)
    stream = stream_gather(1, pl.ds(wide_rows, stream_rows - wide_rows), False)
    wide_cols, kv_width_cols = width_query.shape[1], width_kv.shape[1]
    widths = [
        TensorGather(
            p,
            width_query,
            lambda t: query_width.at[:, pl.ds(pl.multiple_of(t * wide_cols, 128), wide_cols)],
            width_sems.at[0],
            local_sems.at[2],
        ),
        TensorGather(
            p,
            width_kv,
            lambda t: kv_width.at[
                :, pl.ds(pl.multiple_of(t * kv_width_cols, 128), kv_width_cols)
            ],
            width_sems.at[1],
            local_sems.at[3],
        ),
    ]
    for one in widths:
        one.start()
    wide_stream.start()
    stream.start_z()

    @pl.when(p.z == 0)
    def _():
        up[...] = jnp.zeros(up.shape, up.dtype)

    @pl.when(p.z == count - 1)
    def _():
        down[...] = jnp.zeros(down.shape, down.dtype)

    for load in loads:
        load.wait()

    step_rows = 32

    def ring(direction, distance, part):
        window = pl.ds(part * part_rows, part_rows)
        target = p.section + 2 if direction == 0 else p.section - 2
        slot = p.z + distance - 1 if direction == 0 else p.z - distance
        return remote(
            sums.at[slot, window],
            (up, down)[direction].at[distance - 1, window],
            ring_sems.at[direction, 0, distance - 1, part],
            ring_sems.at[direction, 1, distance - 1, part],
            "section",
            target,
        )

    def ring_arrived(direction, distance, part):
        slot = (up, down)[direction].at[distance - 1, pl.ds(part * part_rows, part_rows)]
        remote(
            slot,
            slot,
            ring_sems.at[direction, 0, distance - 1, part],
            ring_sems.at[direction, 1, distance - 1, part],
            "section",
            p.other_x,
        ).wait_recv()

    def pair_sum(far, window):
        value = held[far, window, :].astype(jnp.float32) * factor
        return value + peer[far, window, :].astype(jnp.float32) * peer_factor

    def relay(direction, distance, part):
        slots = (up, down)[direction]
        far = p.z + distance if direction == 0 else p.z - distance
        slot = p.z + distance - 1 if direction == 0 else p.z - distance
        sends = far < count if direction == 0 else far >= 0
        receives = p.z > 0 if direction == 0 else p.z < count - 1

        @pl.when(sends)
        def _():
            if distance < count - 1:

                @pl.when(receives)
                def _():
                    ring_arrived(direction, distance + 1, part)

            @pl.loop(0, part_rows // step_rows)
            def _(i):
                window = pl.ds(
                    pl.multiple_of(part * part_rows + i * step_rows, step_rows), step_rows
                )
                value = pair_sum(far, window)
                if distance < count - 1:
                    value += slots[distance, window, :]
                sums[slot, window, :] = value

            if distance < count - 1:
                beyond = far + 1 < count if direction == 0 else far - 1 >= 0

                @pl.when(beyond)
                def _():
                    ring(direction, distance + 1, part).wait_send()

            ring(direction, distance, part).start()

    for distance in range(count - 1, 0, -1):
        at_distance(distance, pair_arrived)
        at_distance(distance - 1, send_pair)
        if distance == 1:
            stream.start_x()
        for part in range(PARTS):
            relay(0, distance, part)
            relay(1, distance, part)
        if distance == count - 1:
            wide_stream.cross()
        if distance == min(2, count - 1):
            for one in widths:
                one.forward()
            wide_stream.step(1)
            stream.step(1)
    for hop in range(2, count - 1):
        wide_stream.step(hop)
        stream.step(hop)
    at_distance(0, pair_arrived)

    gathers = []
    for part in range(PARTS):

        @pl.when(p.z > 0)
        def _():
            ring_arrived(0, 1, part)

        @pl.when(p.z < count - 1)
        def _():
            ring_arrived(1, 1, part)

        @pl.loop(0, part_rows // step_rows)
        def _(i):
            window = pl.ds(pl.multiple_of(part * part_rows + i * step_rows, step_rows), step_rows)
            value = pair_sum(p.z, window) + up[0, window, :] + down[0, window, :]
            mine[window, :] = value.astype(jnp.bfloat16)

        window = pl.ds(part * part_rows, part_rows)
        for i, (ref, first, width) in enumerate(
            (
                (mixed_query, 0, q_cols),
                (mixed_key, q_cols, k_cols),
                (mixed_value, q_cols + k_cols, k_cols),
            )
        ):
            gather = SectionGather(
                p,
                mine.at[window, pl.ds(first, width)],
                lambda s, ref=ref, width=width, window=window: ref.at[
                    window, pl.ds(pl.multiple_of(s * width, 128), width)
                ],
                mixed_sems.at[3 * part + i],
                local_sems.at[4 + 3 * part + i],
                wide=i == 0 and part == 0,
            )
            gather.start()
            gathers.append(gather)
    if count > 2:
        wide_stream.step(count - 1)
        stream.step(count - 1)
    for gather in gathers:
        gather.cross()
    for hop in range(1, count):
        for gather in gathers:
            gather.step(hop)

    for far in range(count):
        for one in pair_copies(far):
            one.wait_send()
    for part in range(PARTS):

        @pl.when(p.z < count - 1)
        def _():
            ring(0, 1, part).wait_send()

        @pl.when(p.z > 0)
        def _():
            ring(1, 1, part).wait_send()

    wide_stream.finish()
    stream.finish()
    for one in widths:
        one.finish()
    for gather in gathers:
        gather.finish()


def spread_kernel(
    sections,
    expanded,
    hidden,
    whole,
    all_hidden,
    expanded_sems,
    hidden_sems,
    local_sems,
):
    p = Place(sections)
    rows, tokens = expanded.shape[0], hidden.shape[0]
    wide = TensorGather(
        p,
        expanded,
        lambda t: whole.at[pl.ds(pl.multiple_of(t * rows, 16), rows)],
        expanded_sems,
        local_sems.at[0],
    )
    wide_tokens = tokens // 8
    states = [
        SectionGather(
            p,
            hidden.at[pl.ds(first, size)],
            lambda s, first=first, size=size: all_hidden.at[
                pl.ds(pl.multiple_of(s * tokens + first, 16), size)
            ],
            hidden_sems.at[index],
            local_sems.at[1 + index],
            wide=index == 0,
        )
        for index, (first, size) in enumerate(
            ((0, wide_tokens), (wide_tokens, tokens - wide_tokens))
        )
    ]
    wide.start()
    for one in states:
        one.start()
    for one in states:
        one.cross()
    for hop in range(1, p.count):
        for one in states:
            one.step(hop)
    wide.forward()
    for one in states:
        one.finish()
    wide.finish()


def sum_kernel(
    sections,
    partial,
    queries,
    joint,
    near,
    from_core,
    y_out,
    y_in,
    own,
    near_sems,
    core_sems,
    y_sems,
    own_y_sems,
    joint_sems,
    local_sems,
    side_sems,
):
    p = Place(sections)
    rows = near.shape[1]
    q_cols = queries.shape[1]
    joint_cols = own.shape[1]
    spans = ((q_cols, joint_cols), (0, q_cols))

    def core_copy(span, row_y):
        first, width = spans[span]
        block = row_y * 2 + 1 - p.core
        return remote(
            partial.at[pl.ds(pl.multiple_of(block * rows, 16), rows), pl.ds(first, width)],
            from_core.at[row_y, :, pl.ds(first, width)],
            core_sems.at[0, span, row_y],
            core_sems.at[1, span, row_y],
            "tensor",
            p.other_core,
        )

    def near_copy(span, row_y):
        first, width = spans[span]
        block = row_y * 2 + p.core
        return pltpu.make_async_copy(
            partial.at[pl.ds(pl.multiple_of(block * rows, 16), rows), pl.ds(first, width)],
            near.at[row_y, :, pl.ds(first, width)],
            near_sems.at[span, row_y],
        )

    def y_copy(span):
        first, width = spans[span]
        return remote(
            y_out.at[:, pl.ds(first, width)],
            y_in.at[:, pl.ds(first, width)],
            y_sems.at[0, span],
            y_sems.at[1, span],
            "tensor",
            p.other_y,
        )

    step_rows = 32

    def each_window(body):
        @pl.loop(0, rows // step_rows)
        def _(i):
            body(pl.ds(pl.multiple_of(i * step_rows, step_rows), step_rows))

    def core_sum(span, row_y, window):
        first, width = spans[span]
        columns = pl.ds(first, width)
        return near[row_y, window, columns] + from_core[row_y, window, columns]

    def send_sum(span):
        first, width = spans[span]
        near_copy(span, 1 - p.y).wait()
        core_copy(span, 1 - p.y).wait_recv()

        def body(window):
            y_out[window, pl.ds(first, width)] = core_sum(span, 1 - p.y, window).astype(
                jnp.bfloat16
            )

        each_window(body)
        y_copy(span).start()

    def take_sum(span, target):
        first, width = spans[span]
        near_copy(span, p.y).wait()
        core_copy(span, p.y).wait_recv()
        y_copy(span).wait_recv()

        def body(window):
            value = core_sum(span, p.y, window)
            value += y_in[window, pl.ds(first, width)].astype(jnp.float32)
            target[window, :] = value.astype(jnp.bfloat16)

        each_window(body)

    for span in range(2):
        for row_y in (1 - p.y, p.y):
            core_copy(span, row_y).start()
            near_copy(span, row_y).start()

    def block(t, s):
        return joint.at[
            pl.ds(pl.multiple_of(t * rows, 16), rows),
            pl.ds(pl.multiple_of(s * joint_cols, 128), joint_cols),
        ]

    def side(row_y, core, s, src):
        return remote(
            src,
            block(row_y * 2 + core, s),
            side_sems.at[row_y, 0, s],
            side_sems.at[row_y, 1, s],
            "tensor",
            p.other_core,
        )

    def hand_on(row_y):
        def act(s):
            side(row_y, p.core, s, block(row_y * 2 + p.core, s)).start()

        return act

    send_sum(0)
    take_sum(0, own)
    own_y = remote(
        own,
        block(p.tensor, p.section),
        own_y_sems.at[0],
        own_y_sems.at[1],
        "tensor",
        p.other_y,
    )
    own_y.start()
    near_gather = SectionGather(
        p, own, lambda s: block(p.tensor, s), joint_sems.at[0], local_sems.at[0], hand_on(p.y)
    )
    far_gather = SectionGather(
        p, None, lambda s: block(p.other_y, s), joint_sems.at[1], None, hand_on(1 - p.y)
    )
    near_gather.start()
    side(p.y, p.core, p.section, own).start()
    own_y.wait_recv()
    far_gather.start()
    side(1 - p.y, p.core, p.section, block(p.other_y, p.section)).start()
    send_sum(1)
    for hop in range(1, p.count):
        near_gather.step(hop)
        far_gather.step(hop)
    take_sum(1, queries)
    near_gather.finish()
    far_gather.finish()

    @pl.loop(0, sections)
    def _(s):
        for row_y in range(2):
            from_other = block(row_y * 2 + 1 - p.core, s)
            side(row_y, 1 - p.core, s, from_other).wait_recv()
            side(row_y, p.core, s, block(row_y * 2 + p.core, s)).wait_send()

    own_y.wait_send()
    for span in range(2):
        y_copy(span).wait_send()
        for row_y in (1 - p.y, p.y):
            core_copy(span, row_y).wait_send()


def attend_kernel(first, queries, joint, attended):
    rows = queries.shape[0]
    tensor_index = first[0]
    query = queries[...]
    scale = 1.0 / math.sqrt(HD)

    def scores_of(index):
        keys = joint[pl.ds(pl.multiple_of(index * rows, 128), rows), :HD]
        return contract_last(query, keys) * scale

    def merge(index, scores, carry):
        top, bottom, running = carry
        best = jnp.maximum(top, jnp.max(scores, axis=1, keepdims=True))
        weights = jnp.exp(scores - best)
        shrink = jnp.exp(top - best)
        values = joint[pl.ds(pl.multiple_of(index * rows, 128), rows), HD:]
        bottom = bottom * shrink + jnp.sum(weights, axis=1, keepdims=True)
        running = running * shrink + jnp.dot(
            weights.astype(jnp.bfloat16), values, preferred_element_type=jnp.float32
        )
        return best, bottom, running

    scores = scores_of(tensor_index)
    row_of = lax.broadcasted_iota(jnp.int32, (rows, rows), 0)
    column_of = lax.broadcasted_iota(jnp.int32, (rows, rows), 1)
    scores = jnp.where(column_of <= row_of, scores, -jnp.inf)
    top = jnp.max(scores, axis=1, keepdims=True)
    weights = jnp.exp(scores - top)
    values = joint[pl.ds(pl.multiple_of(tensor_index * rows, 128), rows), HD:]
    bottom = jnp.sum(weights, axis=1, keepdims=True)
    running = jnp.dot(weights.astype(jnp.bfloat16), values, preferred_element_type=jnp.float32)
    top, bottom, running = lax.fori_loop(
        0,
        tensor_index,
        lambda index, carry: merge(index, scores_of(index), carry),
        (top, bottom, running),
    )
    attended[...] = (running / bottom).astype(jnp.bfloat16)


def attend(queries, joint, tensor_index):
    rows, cols = queries.shape
    tokens = joint.shape[0]
    return pl.pallas_call(
        attend_kernel,
        out_shape=jax.ShapeDtypeStruct((rows, cols), jnp.bfloat16),
        grid_spec=pltpu.PrefetchScalarGridSpec(
            num_scalar_prefetch=1,
            grid=(cols // HD,),
            in_specs=[
                pl.BlockSpec((rows, HD), lambda h, first: (0, h)),
                pl.BlockSpec((tokens, 2 * HD), lambda h, first: (0, h % KVH)),
            ],
            out_specs=pl.BlockSpec((rows, HD), lambda h, first: (0, h)),
        ),
        compiler_params=pltpu.CompilerParams(vmem_limit_bytes=40 * MIB),
    )(tensor_index.reshape(1).astype(jnp.int32), queries, joint)


def fast_device(
    old_query, old_key, old_value, depth_mix, width_query, width_kv, width_stream, hidden
):
    sections = lax.axis_size("section")
    tensors = lax.axis_size("tensor")
    count = sections // 2
    bf16 = jnp.bfloat16
    dma = pltpu.SemaphoreType.DMA
    rows, model_cols = old_query.shape[1:]
    kv_cols = old_key.shape[2]
    seg = (model_cols + 2 * kv_cols) // sections
    stream_rows, stream_cols = width_stream.shape
    head_cols = width_query.shape[0]
    kv_head_cols = width_kv.shape[0]

    mixed_query, mixed_key, mixed_value, query_width, kv_width, fragment = pl.pallas_call(
        functools.partial(mix_kernel, sections),
        out_shape=[
            jax.ShapeDtypeStruct((rows, model_cols), bf16),
            jax.ShapeDtypeStruct((rows, kv_cols), bf16),
            jax.ShapeDtypeStruct((rows, kv_cols), bf16),
            jax.ShapeDtypeStruct((head_cols, model_cols), bf16),
            jax.ShapeDtypeStruct((kv_head_cols, kv_cols), bf16),
            jax.ShapeDtypeStruct((stream_rows, stream_cols * sections), bf16),
        ],
        in_specs=[pl.BlockSpec(memory_space=pltpu.SMEM)] + [ANY] * 6,
        out_specs=[ANY] * 6,
        scratch_shapes=[
            pltpu.VMEM((count, rows, seg), bf16),
            pltpu.VMEM((count, rows, seg), bf16),
            pltpu.VMEM((count - 1, rows, seg), jnp.float32),
            pltpu.VMEM((count - 1, rows, seg), jnp.float32),
            pltpu.VMEM((count - 1, rows, seg), jnp.float32),
            pltpu.VMEM((rows, seg), bf16),
            dma((3 * count,)),
            dma((2, count, 3)),
            dma((2, 2, count - 1, PARTS)),
            dma((3 * PARTS, 4, sections)),
            dma((2, 4, sections)),
            dma((2, 6)),
            dma((4 + 3 * PARTS,)),
        ],
        compiler_params=pltpu.CompilerParams(
            vmem_limit_bytes=52 * MIB, has_side_effects=True
        ),
    )(depth_mix, old_query[0], old_key[0], old_value[0], width_query, width_kv, width_stream)

    expanded = jnp.concatenate(
        [
            contract_last(mixed_query, query_width).astype(bf16),
            contract_last(mixed_key, kv_width).astype(bf16),
            contract_last(mixed_value, kv_width).astype(bf16),
        ],
        axis=1,
    )
    joined_cols = expanded.shape[1]
    token_part, feature_cols = hidden.shape
    tokens = token_part * sections

    whole, all_hidden = pl.pallas_call(
        functools.partial(spread_kernel, sections),
        out_shape=[
            jax.ShapeDtypeStruct((rows * tensors, joined_cols), bf16),
            jax.ShapeDtypeStruct((tokens, feature_cols), bf16),
        ],
        in_specs=[ANY] * 2,
        out_specs=[ANY] * 2,
        scratch_shapes=[dma((6,)), dma((2, 4, sections)), dma((3,))],
        compiler_params=pltpu.CompilerParams(
            vmem_limit_bytes=16 * MIB, has_side_effects=True
        ),
    )(expanded, hidden)

    grown = jnp.dot(fragment, whole, preferred_element_type=jnp.float32).astype(bf16)
    partial = jnp.dot(all_hidden, grown, preferred_element_type=jnp.float32)
    block_rows = tokens // tensors
    queries, joint = pl.pallas_call(
        functools.partial(sum_kernel, sections),
        out_shape=[
            jax.ShapeDtypeStruct((block_rows, head_cols), bf16),
            jax.ShapeDtypeStruct((tokens, 2 * kv_head_cols * sections), bf16),
        ],
        in_specs=[ANY],
        out_specs=[pl.BlockSpec(memory_space=pltpu.VMEM), ANY],
        scratch_shapes=[
            pltpu.VMEM((2, block_rows, joined_cols), jnp.float32),
            pltpu.VMEM((2, block_rows, joined_cols), jnp.float32),
            pltpu.VMEM((block_rows, joined_cols), bf16),
            pltpu.VMEM((block_rows, joined_cols), bf16),
            pltpu.VMEM((block_rows, 2 * kv_head_cols), bf16),
            dma((2, 2)),
            dma((2, 2, 2)),
            dma((2, 2)),
            dma((2,)),
            dma((2, 4, sections)),
            dma((1,)),
            dma((2, 2, sections)),
        ],
        compiler_params=pltpu.CompilerParams(
            vmem_limit_bytes=32 * MIB, has_side_effects=True
        ),
    )(partial)

    attended = attend(queries, joint, lax.axis_index("tensor"))
    return (
        grown[:, :head_cols],
        grown[:, head_cols : head_cols + kv_head_cols],
        grown[:, head_cols + kv_head_cols :],
        attended,
    )


def mix_layers(depth_mix, stacked):
    flattened = stacked.reshape(stacked.shape[0], -1)
    mixed = jnp.dot(
        depth_mix, flattened, precision=lax.Precision.HIGHEST, preferred_element_type=jnp.float32
    )
    return mixed.reshape(stacked.shape[1:]).astype(jnp.bfloat16)


def pick_heads(wide, kv_ids):
    row_count = wide.shape[0]
    grouped = wide.reshape(row_count, KVH, HD)
    chosen = jnp.take(grouped, kv_ids, axis=1)
    return chosen.reshape(row_count, kv_ids.shape[0] * HD)


def plain_device(
    old_query, old_key, old_value, depth_mix, width_query, width_kv, width_stream, hidden
):
    section_index = lax.axis_index("section")
    tensor_index = lax.axis_index("tensor")
    tensor_count = lax.axis_size("tensor")
    moved_query, moved_key, moved_value = (
        lax.all_to_all(old_query, "section", split_axis=2, concat_axis=0, tiled=True),
        lax.all_to_all(old_key, "section", split_axis=2, concat_axis=0, tiled=True),
        lax.all_to_all(old_value, "section", split_axis=2, concat_axis=0, tiled=True),
    )
    part_query = mix_layers(depth_mix, moved_query)
    part_key = mix_layers(depth_mix, moved_key)
    part_value = mix_layers(depth_mix, moved_value)
    mixed_query, mixed_key, mixed_value = (
        lax.all_gather(part_query, "section", axis=1, tiled=True),
        lax.all_gather(part_key, "section", axis=1, tiled=True),
        lax.all_gather(part_value, "section", axis=1, tiled=True),
    )
    query_width, kv_width = (
        lax.all_gather(width_query, "tensor", axis=1, tiled=True),
        lax.all_gather(width_kv, "tensor", axis=1, tiled=True),
    )
    expanded_query = contract_last(mixed_query, query_width).astype(jnp.bfloat16)
    expanded_key = contract_last(mixed_key, kv_width).astype(jnp.bfloat16)
    expanded_value = contract_last(mixed_value, kv_width).astype(jnp.bfloat16)
    whole_query, whole_key, whole_value = (
        lax.all_gather(expanded_query, "tensor", axis=0, tiled=True),
        lax.all_gather(expanded_key, "tensor", axis=0, tiled=True),
        lax.all_gather(expanded_value, "tensor", axis=0, tiled=True),
    )
    fragment = lax.all_gather(width_stream, "section", axis=1, tiled=True)

    def product_of(whole):
        return jnp.dot(fragment, whole, preferred_element_type=jnp.float32)

    sum_query = product_of(whole_query)
    sum_key = product_of(whole_key)
    sum_value = product_of(whole_value)
    grown_query = sum_query.astype(jnp.bfloat16)
    grown_key = sum_key.astype(jnp.bfloat16)
    grown_value = sum_value.astype(jnp.bfloat16)
    all_hidden = lax.all_gather(hidden, "section", axis=0, tiled=True)
    token_count = all_hidden.shape[0]
    block_rows = token_count // tensor_count
    query_cols = grown_query.shape[1]
    heads_here = query_cols // HD
    head_ids = section_index * heads_here + jnp.arange(heads_here, dtype=jnp.int32)
    kv_ids = head_ids % KVH
    joined = jnp.concatenate([grown_query, grown_key, grown_value], axis=1)
    summed = lax.psum_scatter(
        jnp.dot(all_hidden, joined, preferred_element_type=jnp.float32),
        "tensor",
        scatter_dimension=0,
        tiled=True,
    )
    kv_cols = (summed.shape[1] - query_cols) // 2
    queries = summed[:, :query_cols].astype(jnp.bfloat16)
    key_part = summed[:, query_cols : query_cols + kv_cols].astype(jnp.bfloat16)
    value_part = summed[:, query_cols + kv_cols :].astype(jnp.bfloat16)
    key_wide, value_wide = (
        lax.all_gather(key_part, "section", axis=1, tiled=True),
        lax.all_gather(value_part, "section", axis=1, tiled=True),
    )
    key_here = pick_heads(key_wide, kv_ids)
    value_here = pick_heads(value_wide, kv_ids)
    key_rows, value_rows = (
        lax.all_gather(key_here, "tensor", axis=0, tiled=True),
        lax.all_gather(value_here, "tensor", axis=0, tiled=True),
    )
    query_heads = queries.reshape(block_rows, heads_here, HD)
    key_heads = key_rows.reshape(token_count, heads_here, HD)
    value_heads = value_rows.reshape(token_count, heads_here, HD)
    scores = jnp.einsum(
        "qhd,khd->hqk", query_heads, key_heads, preferred_element_type=jnp.float32
    ) * (1.0 / math.sqrt(HD))
    query_position = tensor_index * block_rows + lax.broadcasted_iota(jnp.int32, (block_rows, 1), 0)
    key_position = lax.broadcasted_iota(jnp.int32, (1, token_count), 1)
    scores = jnp.where((key_position <= query_position)[None], scores, -jnp.inf)
    row_max = jnp.max(scores, axis=2, keepdims=True)
    weights = jnp.exp(scores - row_max)
    denominator = jnp.sum(weights, axis=2, keepdims=True)
    probs = weights.astype(jnp.bfloat16)
    mixed_out = (
        jnp.einsum("hqk,khd->hqd", probs, value_heads, preferred_element_type=jnp.float32)
        / denominator
    )
    attended = (
        jnp.transpose(mixed_out, (1, 0, 2))
        .reshape(block_rows, heads_here * HD)
        .astype(jnp.bfloat16)
    )
    return (grown_query, grown_key, grown_value, attended)


def fits(mesh):
    sections, tensors = mesh.shape["section"], mesh.shape["tensor"]
    return sections == KVH and tensors == 4


def solution(mesh):
    placed = (
        P("section", "tensor", None),
        P("section", "tensor", None),
        P("section", "tensor", None),
        P(),
        P("section", "tensor"),
        P("section", "tensor"),
        P("tensor", "section"),
        P("section", "tensor"),
    )
    return jax.shard_map(
        fast_device if fits(mesh) else plain_device,
        mesh=mesh,
        in_specs=placed,
        out_specs=(
            P("tensor", "section"),
            P("tensor", "section"),
            P("tensor", "section"),
            P("tensor", "section"),
        ),
        check_vma=False,
    )
```

```python
import functools
import math

import jax
import jax.numpy as jnp
from jax import lax
from jax.experimental import pallas as pl
from jax.experimental.pallas import tpu as pltpu
from jax.sharding import PartitionSpec as P

HD = 128
KVH = 8
MIB = 1024 * 1024
ANY = pl.BlockSpec(memory_space=pl.ANY)


def contract_last(left_side, right_side):
    return lax.dot_general(
        left_side, right_side, (((1,), (1,)), ((), ())), preferred_element_type=jnp.float32
    )


def remote(src, dst, send, recv, axis, index):
    return pltpu.make_async_remote_copy(
        src_ref=src,
        dst_ref=dst,
        send_sem=send,
        recv_sem=recv,
        device_id={axis: index},
        device_id_type=pl.DeviceIdType.MESH,
    )


class Place:
    def __init__(self, sections):
        self.count = sections // 2
        self.section = lax.axis_index("section")
        self.tensor = lax.axis_index("tensor")
        self.z = self.section // 2
        self.x = self.section % 2
        self.y = self.tensor // 2
        self.core = self.tensor % 2
        self.other_x = self.z * 2 + 1 - self.x
        self.other_y = (1 - self.y) * 2 + self.core
        self.other_core = self.y * 2 + 1 - self.core


class SectionGather:
    def __init__(self, place, own, view, sems, local_sem=None, on_block=None, wide=False):
        self.p = place
        self.own = view(place.section) if own is None else own
        self.view = view
        self.sems = sems
        self.local = None
        if local_sem is not None:
            self.local = pltpu.make_async_copy(self.own, view(place.section), local_sem)
        self.on_block = on_block
        self.wide = wide

    def copy(self, kind, origin, src):
        p = self.p
        target = (p.section + 2, p.section - 2, p.other_x)[kind - 1]
        return remote(
            src,
            self.view(origin),
            self.sems.at[kind, origin],
            self.sems.at[0, origin],
            "section",
            target,
        )

    def start_z(self):
        p = self.p

        @pl.when(p.z < p.count - 1)
        def _():
            self.copy(1, p.section, self.own).start()

        @pl.when(p.z > 0)
        def _():
            self.copy(2, p.section, self.own).start()

        if self.local is not None:
            self.local.start()

    def start_x(self):
        self.copy(3, self.p.section, self.own).start()

    def start(self):
        if self.wide:
            self.start_x()
            self.start_z()
        else:
            self.start_z()
            self.start_x()

    def arrived(self, origin):
        self.copy(3, origin, self.view(origin)).wait_recv()

    def cross(self):
        p = self.p
        if self.wide:
            origin = p.other_x
            block = self.view(origin)
            self.arrived(origin)

            @pl.when(p.z < p.count - 1)
            def _():
                self.copy(1, origin, block).start()

            @pl.when(p.z > 0)
            def _():
                self.copy(2, origin, block).start()

    def step(self, hop):
        p = self.p

        def take(origin, kind, more):
            block = self.view(origin)
            self.arrived(origin)

            @pl.when(more)
            def _():
                self.copy(kind, origin, block).start()

            if not self.wide:
                self.copy(3, origin, block).start()
            if self.on_block is not None:
                self.on_block(origin)

        columns = (p.section, p.other_x) if self.wide else (p.section,)

        @pl.when(p.z - hop >= 0)
        def _():
            for column in columns:
                take(column - 2 * hop, 1, p.z < p.count - 1)

        @pl.when(p.z + hop < p.count)
        def _():
            for column in columns:
                take(column + 2 * hop, 2, p.z > 0)

    def finish(self):
        p = self.p
        if self.local is not None:
            self.local.wait()
        if not self.wide:
            for other_z in range(p.count):
                across = other_z * 2 + 1 - p.x
                self.arrived(across)
                if self.on_block is not None:
                    self.on_block(across)
        for other_z in range(p.count):
            for column in (p.x, 1 - p.x) if self.wide else (p.x,):
                origin = other_z * 2 + column
                block = self.view(origin)

                @pl.when((other_z <= p.z) & (p.z < p.count - 1))
                def _():
                    self.copy(1, origin, block).wait_send()

                @pl.when((other_z >= p.z) & (p.z > 0))
                def _():
                    self.copy(2, origin, block).wait_send()

            if not self.wide:
                self.copy(3, origin, block).wait_send()
        if self.wide:
            self.copy(3, p.section, self.own).wait_send()


class TensorGather:
    def __init__(self, place, own, view, sems, local_sem):
        p = place
        mine, far = p.tensor, p.other_y
        self.local = pltpu.make_async_copy(own, view(mine), local_sem)
        self.to_y = remote(own, view(mine), sems.at[0], sems.at[1], "tensor", p.other_y)
        self.to_core = remote(own, view(mine), sems.at[2], sems.at[3], "tensor", p.other_core)
        self.far_to_core = remote(
            view(far), view(far), sems.at[4], sems.at[5], "tensor", p.other_core
        )

    def start(self):
        self.to_y.start()
        self.to_core.start()
        self.local.start()

    def forward(self):
        self.to_y.wait_recv()
        self.far_to_core.start()

    def finish(self):
        self.local.wait()
        self.to_y.wait_send()
        self.to_core.wait()
        self.far_to_core.wait()


PARTS = 2


def mix_kernel(
    sections,
    depth_mix,
    old_query,
    old_key,
    old_value,
    width_query,
    width_kv,
    width_stream,
    mixed_query,
    mixed_key,
    mixed_value,
    query_width,
    kv_width,
    fragment,
    held,
    peer,
    sums,
    up,
    down,
    mine,
    load_sems,
    pair_sems,
    ring_sems,
    mixed_sems,
    stream_sems,
    width_sems,
    local_sems,
):
    p = Place(sections)
    count = p.count
    rows = held.shape[1]
    part_rows = rows // PARTS
    q_cols = old_query.shape[1] // sections
    k_cols = old_key.shape[1] // sections
    fields = (
        (old_query, 0, q_cols),
        (old_key, q_cols, k_cols),
        (old_value, q_cols + k_cols, k_cols),
    )
    factor = depth_mix[p.section]
    peer_factor = depth_mix[p.other_x]

    def pair_copies(far):
        for i, (ref, first, width) in enumerate(fields):
            start = pl.multiple_of((far * 2 + 1 - p.x) * width, 128)
            yield remote(
                ref.at[:, pl.ds(start, width)],
                peer.at[far, :, pl.ds(first, width)],
                pair_sems.at[0, far, i],
                pair_sems.at[1, far, i],
                "section",
                p.other_x,
            )

    def at_distance(distance, act):
        @pl.when(p.z + distance < count)
        def _():
            act(p.z + distance)

        if distance:

            @pl.when(p.z - distance >= 0)
            def _():
                act(p.z - distance)

    def send_pair(far):
        for one in pair_copies(far):
            one.start()

    def pair_arrived(far):
        for one in pair_copies(far):
            one.wait_recv()

    at_distance(count - 1, send_pair)

    loads = []
    for far in range(count):
        for i, (ref, first, width) in enumerate(fields):
            start = pl.multiple_of((far * 2 + p.x) * width, 128)
            load = pltpu.make_async_copy(
                ref.at[:, pl.ds(start, width)],
                held.at[far, :, pl.ds(first, width)],
                load_sems.at[3 * far + i],
            )
            load.start()
            loads.append(load)

    stream_rows, stream_cols = width_stream.shape
    wide_rows = stream_rows // 4

    def stream_gather(index, window, wide):
        return SectionGather(
            p,
            width_stream.at[window],
            lambda s: fragment.at[
                window, pl.ds(pl.multiple_of(s * stream_cols, 128), stream_cols)
            ],
            stream_sems.at[index],
            local_sems.at[index],
            wide=wide,
        )

    wide_stream = stream_gather(0, pl.ds(0, wide_rows), True)
    stream = stream_gather(1, pl.ds(wide_rows, stream_rows - wide_rows), False)
    wide_cols, kv_width_cols = width_query.shape[1], width_kv.shape[1]
    widths = [
        TensorGather(
            p,
            width_query,
            lambda t: query_width.at[:, pl.ds(pl.multiple_of(t * wide_cols, 128), wide_cols)],
            width_sems.at[0],
            local_sems.at[2],
        ),
        TensorGather(
            p,
            width_kv,
            lambda t: kv_width.at[
                :, pl.ds(pl.multiple_of(t * kv_width_cols, 128), kv_width_cols)
            ],
            width_sems.at[1],
            local_sems.at[3],
        ),
    ]
    for one in widths:
        one.start()
    wide_stream.start()
    stream.start_z()

    @pl.when(p.z == 0)
    def _():
        up[...] = jnp.zeros(up.shape, up.dtype)

    @pl.when(p.z == count - 1)
    def _():
        down[...] = jnp.zeros(down.shape, down.dtype)

    for load in loads:
        load.wait()

    step_rows = 32

    def ring(direction, distance, part):
        window = pl.ds(part * part_rows, part_rows)
        target = p.section + 2 if direction == 0 else p.section - 2
        slot = p.z + distance - 1 if direction == 0 else p.z - distance
        return remote(
            sums.at[slot, window],
            (up, down)[direction].at[distance - 1, window],
            ring_sems.at[direction, 0, distance - 1, part],
            ring_sems.at[direction, 1, distance - 1, part],
            "section",
            target,
        )

    def ring_arrived(direction, distance, part):
        slot = (up, down)[direction].at[distance - 1, pl.ds(part * part_rows, part_rows)]
        remote(
            slot,
            slot,
            ring_sems.at[direction, 0, distance - 1, part],
            ring_sems.at[direction, 1, distance - 1, part],
            "section",
            p.other_x,
        ).wait_recv()

    def pair_sum(far, window):
        value = held[far, window, :].astype(jnp.float32) * factor
        return value + peer[far, window, :].astype(jnp.float32) * peer_factor

    def relay(direction, distance, part):
        slots = (up, down)[direction]
        far = p.z + distance if direction == 0 else p.z - distance
        slot = p.z + distance - 1 if direction == 0 else p.z - distance
        sends = far < count if direction == 0 else far >= 0
        receives = p.z > 0 if direction == 0 else p.z < count - 1

        @pl.when(sends)
        def _():
            if distance < count - 1:

                @pl.when(receives)
                def _():
                    ring_arrived(direction, distance + 1, part)

            @pl.loop(0, part_rows // step_rows)
            def _(i):
                window = pl.ds(
                    pl.multiple_of(part * part_rows + i * step_rows, step_rows), step_rows
                )
                value = pair_sum(far, window)
                if distance < count - 1:
                    value += slots[distance, window, :]
                sums[slot, window, :] = value

            if distance < count - 1:
                beyond = far + 1 < count if direction == 0 else far - 1 >= 0

                @pl.when(beyond)
                def _():
                    ring(direction, distance + 1, part).wait_send()

            ring(direction, distance, part).start()

    for distance in range(count - 1, 0, -1):
        at_distance(distance, pair_arrived)
        at_distance(distance - 1, send_pair)
        if distance == 1:
            stream.start_x()
        for part in range(PARTS):
            relay(0, distance, part)
            relay(1, distance, part)
        if distance == count - 1:
            wide_stream.cross()
        if distance == min(2, count - 1):
            for one in widths:
                one.forward()
            wide_stream.step(1)
            stream.step(1)
    for hop in range(2, count - 1):
        wide_stream.step(hop)
        stream.step(hop)
    at_distance(0, pair_arrived)

    gathers = []
    for part in range(PARTS):

        @pl.when(p.z > 0)
        def _():
            ring_arrived(0, 1, part)

        @pl.when(p.z < count - 1)
        def _():
            ring_arrived(1, 1, part)

        @pl.loop(0, part_rows // step_rows)
        def _(i):
            window = pl.ds(pl.multiple_of(part * part_rows + i * step_rows, step_rows), step_rows)
            value = pair_sum(p.z, window) + up[0, window, :] + down[0, window, :]
            mine[window, :] = value.astype(jnp.bfloat16)

        window = pl.ds(part * part_rows, part_rows)
        for i, (ref, first, width) in enumerate(
            (
                (mixed_query, 0, q_cols),
                (mixed_key, q_cols, k_cols),
                (mixed_value, q_cols + k_cols, k_cols),
            )
        ):
            gather = SectionGather(
                p,
                mine.at[window, pl.ds(first, width)],
                lambda s, ref=ref, width=width, window=window: ref.at[
                    window, pl.ds(pl.multiple_of(s * width, 128), width)
                ],
                mixed_sems.at[3 * part + i],
                local_sems.at[4 + 3 * part + i],
                wide=i == 0 and part == 0,
            )
            gather.start()
            gathers.append(gather)
    if count > 2:
        wide_stream.step(count - 1)
        stream.step(count - 1)
    for gather in gathers:
        gather.cross()
    for hop in range(1, count):
        for gather in gathers:
            gather.step(hop)

    for far in range(count):
        for one in pair_copies(far):
            one.wait_send()
    for part in range(PARTS):

        @pl.when(p.z < count - 1)
        def _():
            ring(0, 1, part).wait_send()

        @pl.when(p.z > 0)
        def _():
            ring(1, 1, part).wait_send()

    wide_stream.finish()
    stream.finish()
    for one in widths:
        one.finish()
    for gather in gathers:
        gather.finish()


def spread_kernel(sections, expanded, whole, expanded_sems, local_sems):
    p = Place(sections)
    rows = expanded.shape[0]
    wide = TensorGather(
        p,
        expanded,
        lambda t: whole.at[pl.ds(pl.multiple_of(t * rows, 16), rows)],
        expanded_sems,
        local_sems.at[0],
    )
    wide.start()
    wide.forward()
    wide.finish()


def sum_kernel(
    sections,
    partial,
    queries,
    joint,
    near,
    from_core,
    y_out,
    y_in,
    own,
    near_sems,
    core_sems,
    y_sems,
    own_y_sems,
    joint_sems,
    local_sems,
    side_sems,
):
    p = Place(sections)
    rows = near.shape[1]
    q_cols = queries.shape[1]
    joint_cols = own.shape[1]
    spans = ((q_cols, joint_cols), (0, q_cols))

    def core_copy(span, row_y):
        first, width = spans[span]
        block = row_y * 2 + 1 - p.core
        return remote(
            partial.at[pl.ds(pl.multiple_of(block * rows, 16), rows), pl.ds(first, width)],
            from_core.at[row_y, :, pl.ds(first, width)],
            core_sems.at[0, span, row_y],
            core_sems.at[1, span, row_y],
            "tensor",
            p.other_core,
        )

    def near_copy(span, row_y):
        first, width = spans[span]
        block = row_y * 2 + p.core
        return pltpu.make_async_copy(
            partial.at[pl.ds(pl.multiple_of(block * rows, 16), rows), pl.ds(first, width)],
            near.at[row_y, :, pl.ds(first, width)],
            near_sems.at[span, row_y],
        )

    def y_copy(span):
        first, width = spans[span]
        return remote(
            y_out.at[:, pl.ds(first, width)],
            y_in.at[:, pl.ds(first, width)],
            y_sems.at[0, span],
            y_sems.at[1, span],
            "tensor",
            p.other_y,
        )

    step_rows = 32

    def each_window(body):
        @pl.loop(0, rows // step_rows)
        def _(i):
            body(pl.ds(pl.multiple_of(i * step_rows, step_rows), step_rows))

    def core_sum(span, row_y, window):
        first, width = spans[span]
        columns = pl.ds(first, width)
        return near[row_y, window, columns] + from_core[row_y, window, columns]

    def send_sum(span):
        first, width = spans[span]
        near_copy(span, 1 - p.y).wait()
        core_copy(span, 1 - p.y).wait_recv()

        def body(window):
            y_out[window, pl.ds(first, width)] = core_sum(span, 1 - p.y, window).astype(
                jnp.bfloat16
            )

        each_window(body)
        y_copy(span).start()

    def take_sum(span, target):
        first, width = spans[span]
        near_copy(span, p.y).wait()
        core_copy(span, p.y).wait_recv()
        y_copy(span).wait_recv()

        def body(window):
            value = core_sum(span, p.y, window)
            value += y_in[window, pl.ds(first, width)].astype(jnp.float32)
            target[window, :] = value.astype(jnp.bfloat16)

        each_window(body)

    for span in range(2):
        for row_y in (1 - p.y, p.y):
            core_copy(span, row_y).start()
            near_copy(span, row_y).start()

    def block(t, s):
        return joint.at[
            pl.ds(pl.multiple_of(t * rows, 16), rows),
            pl.ds(pl.multiple_of(s * joint_cols, 128), joint_cols),
        ]

    def side(row_y, core, s, src):
        return remote(
            src,
            block(row_y * 2 + core, s),
            side_sems.at[row_y, 0, s],
            side_sems.at[row_y, 1, s],
            "tensor",
            p.other_core,
        )

    def hand_on(row_y):
        def act(s):
            side(row_y, p.core, s, block(row_y * 2 + p.core, s)).start()

        return act

    send_sum(0)
    take_sum(0, own)
    own_y = remote(
        own,
        block(p.tensor, p.section),
        own_y_sems.at[0],
        own_y_sems.at[1],
        "tensor",
        p.other_y,
    )
    own_y.start()
    near_gather = SectionGather(
        p, own, lambda s: block(p.tensor, s), joint_sems.at[0], local_sems.at[0], hand_on(p.y)
    )
    far_gather = SectionGather(
        p, None, lambda s: block(p.other_y, s), joint_sems.at[1], None, hand_on(1 - p.y)
    )
    near_gather.start()
    side(p.y, p.core, p.section, own).start()
    own_y.wait_recv()
    far_gather.start()
    side(1 - p.y, p.core, p.section, block(p.other_y, p.section)).start()
    send_sum(1)
    for hop in range(1, p.count):
        near_gather.step(hop)
        far_gather.step(hop)
    take_sum(1, queries)
    near_gather.finish()
    far_gather.finish()

    @pl.loop(0, sections)
    def _(s):
        for row_y in range(2):
            from_other = block(row_y * 2 + 1 - p.core, s)
            side(row_y, 1 - p.core, s, from_other).wait_recv()
            side(row_y, p.core, s, block(row_y * 2 + p.core, s)).wait_send()

    own_y.wait_send()
    for span in range(2):
        y_copy(span).wait_send()
        for row_y in (1 - p.y, p.y):
            core_copy(span, row_y).wait_send()


GROUP = 2


def attend_kernel(first, queries, joint, attended):
    rows = queries.shape[0]
    tensor_index = first[0]
    scale = 1.0 / math.sqrt(HD) / math.log(2.0)

    def span(index):
        return pl.ds(pl.multiple_of(index * rows, 128), rows)

    def scores_of(index, i):
        keys = joint[span(index), 2 * i * HD : (2 * i + 1) * HD]
        return contract_last(queries[:, i * HD : (i + 1) * HD], keys)

    def values_of(index, i):
        return joint[span(index), (2 * i + 1) * HD : (2 * i + 2) * HD]

    def opening(i):
        scores = scores_of(tensor_index, i)
        row_of = lax.broadcasted_iota(jnp.int32, (rows, rows), 0)
        column_of = lax.broadcasted_iota(jnp.int32, (rows, rows), 1)
        scores = jnp.where(column_of <= row_of, scores, -jnp.inf)
        top = jnp.max(scores, axis=1, keepdims=True)
        weights = jnp.exp2((scores - top) * scale)
        bottom = jnp.sum(weights, axis=1, keepdims=True)
        running = jnp.dot(
            weights.astype(jnp.bfloat16),
            values_of(tensor_index, i),
            preferred_element_type=jnp.float32,
        )
        return top, bottom, running

    def merge(index, i, carry):
        top, bottom, running = carry
        scores = scores_of(index, i)
        best = jnp.maximum(top, jnp.max(scores, axis=1, keepdims=True))
        weights = jnp.exp2((scores - best) * scale)
        shrink = jnp.exp2((top - best) * scale)
        bottom = bottom * shrink + jnp.sum(weights, axis=1, keepdims=True)
        running = running * shrink + jnp.dot(
            weights.astype(jnp.bfloat16), values_of(index, i), preferred_element_type=jnp.float32
        )
        return best, bottom, running

    state = lax.fori_loop(
        0,
        tensor_index,
        lambda index, state: tuple(merge(index, i, one) for i, one in enumerate(state)),
        tuple(opening(i) for i in range(GROUP)),
    )
    for i, (_, bottom, running) in enumerate(state):
        attended[:, i * HD : (i + 1) * HD] = (running / bottom).astype(jnp.bfloat16)


def attend(queries, joint, tensor_index):
    rows, cols = queries.shape
    tokens = joint.shape[0]
    return pl.pallas_call(
        attend_kernel,
        out_shape=jax.ShapeDtypeStruct((rows, cols), jnp.bfloat16),
        grid_spec=pltpu.PrefetchScalarGridSpec(
            num_scalar_prefetch=1,
            grid=(cols // (GROUP * HD),),
            in_specs=[
                pl.BlockSpec((rows, GROUP * HD), lambda h, first: (0, h)),
                pl.BlockSpec((tokens, 2 * GROUP * HD), lambda h, first: (0, h % (KVH // GROUP))),
            ],
            out_specs=pl.BlockSpec((rows, GROUP * HD), lambda h, first: (0, h)),
        ),
        compiler_params=pltpu.CompilerParams(vmem_limit_bytes=58 * MIB),
    )(tensor_index.reshape(1).astype(jnp.int32), queries, joint)


def fast_device(
    old_query, old_key, old_value, depth_mix, width_query, width_kv, width_stream, hidden
):
    sections = lax.axis_size("section")
    tensors = lax.axis_size("tensor")
    count = sections // 2
    bf16 = jnp.bfloat16
    dma = pltpu.SemaphoreType.DMA
    rows, model_cols = old_query.shape[1:]
    kv_cols = old_key.shape[2]
    seg = (model_cols + 2 * kv_cols) // sections
    stream_rows, stream_cols = width_stream.shape
    head_cols = width_query.shape[0]
    kv_head_cols = width_kv.shape[0]

    all_hidden = lax.all_gather(hidden, "section", axis=0, tiled=True)
    mixed_query, mixed_key, mixed_value, query_width, kv_width, fragment = pl.pallas_call(
        functools.partial(mix_kernel, sections),
        out_shape=[
            jax.ShapeDtypeStruct((rows, model_cols), bf16),
            jax.ShapeDtypeStruct((rows, kv_cols), bf16),
            jax.ShapeDtypeStruct((rows, kv_cols), bf16),
            jax.ShapeDtypeStruct((head_cols, model_cols), bf16),
            jax.ShapeDtypeStruct((kv_head_cols, kv_cols), bf16),
            jax.ShapeDtypeStruct((stream_rows, stream_cols * sections), bf16),
        ],
        in_specs=[pl.BlockSpec(memory_space=pltpu.SMEM)] + [ANY] * 6,
        out_specs=[ANY] * 6,
        scratch_shapes=[
            pltpu.VMEM((count, rows, seg), bf16),
            pltpu.VMEM((count, rows, seg), bf16),
            pltpu.VMEM((count - 1, rows, seg), jnp.float32),
            pltpu.VMEM((count - 1, rows, seg), jnp.float32),
            pltpu.VMEM((count - 1, rows, seg), jnp.float32),
            pltpu.VMEM((rows, seg), bf16),
            dma((3 * count,)),
            dma((2, count, 3)),
            dma((2, 2, count - 1, PARTS)),
            dma((3 * PARTS, 4, sections)),
            dma((2, 4, sections)),
            dma((2, 6)),
            dma((4 + 3 * PARTS,)),
        ],
        compiler_params=pltpu.CompilerParams(
            vmem_limit_bytes=52 * MIB, has_side_effects=True
        ),
    )(depth_mix, old_query[0], old_key[0], old_value[0], width_query, width_kv, width_stream)

    expanded = jnp.concatenate(
        [
            contract_last(mixed_query, query_width).astype(bf16),
            contract_last(mixed_key, kv_width).astype(bf16),
            contract_last(mixed_value, kv_width).astype(bf16),
        ],
        axis=1,
    )
    joined_cols = expanded.shape[1]
    tokens = all_hidden.shape[0]

    whole = pl.pallas_call(
        functools.partial(spread_kernel, sections),
        out_shape=jax.ShapeDtypeStruct((rows * tensors, joined_cols), bf16),
        in_specs=[ANY],
        out_specs=ANY,
        scratch_shapes=[dma((6,)), dma((1,))],
        compiler_params=pltpu.CompilerParams(
            vmem_limit_bytes=16 * MIB, has_side_effects=True
        ),
    )(expanded)

    grown = jnp.dot(fragment, whole, preferred_element_type=jnp.float32).astype(bf16)
    partial = jnp.dot(all_hidden, grown, preferred_element_type=jnp.float32)
    block_rows = tokens // tensors
    queries, joint = pl.pallas_call(
        functools.partial(sum_kernel, sections),
        out_shape=[
            jax.ShapeDtypeStruct((block_rows, head_cols), bf16),
            jax.ShapeDtypeStruct((tokens, 2 * kv_head_cols * sections), bf16),
        ],
        in_specs=[ANY],
        out_specs=[pl.BlockSpec(memory_space=pltpu.VMEM), ANY],
        scratch_shapes=[
            pltpu.VMEM((2, block_rows, joined_cols), jnp.float32),
            pltpu.VMEM((2, block_rows, joined_cols), jnp.float32),
            pltpu.VMEM((block_rows, joined_cols), bf16),
            pltpu.VMEM((block_rows, joined_cols), bf16),
            pltpu.VMEM((block_rows, 2 * kv_head_cols), bf16),
            dma((2, 2)),
            dma((2, 2, 2)),
            dma((2, 2)),
            dma((2,)),
            dma((2, 4, sections)),
            dma((1,)),
            dma((2, 2, sections)),
        ],
        compiler_params=pltpu.CompilerParams(
            vmem_limit_bytes=56 * MIB, has_side_effects=True
        ),
    )(partial)

    attended = attend(queries, joint, lax.axis_index("tensor"))
    return (
        grown[:, :head_cols],
        grown[:, head_cols : head_cols + kv_head_cols],
        grown[:, head_cols + kv_head_cols :],
        attended,
    )


def mix_layers(depth_mix, stacked):
    flattened = stacked.reshape(stacked.shape[0], -1)
    mixed = jnp.dot(
        depth_mix, flattened, precision=lax.Precision.HIGHEST, preferred_element_type=jnp.float32
    )
    return mixed.reshape(stacked.shape[1:]).astype(jnp.bfloat16)


def pick_heads(wide, kv_ids):
    row_count = wide.shape[0]
    grouped = wide.reshape(row_count, KVH, HD)
    chosen = jnp.take(grouped, kv_ids, axis=1)
    return chosen.reshape(row_count, kv_ids.shape[0] * HD)


def plain_device(
    old_query, old_key, old_value, depth_mix, width_query, width_kv, width_stream, hidden
):
    section_index = lax.axis_index("section")
    tensor_index = lax.axis_index("tensor")
    tensor_count = lax.axis_size("tensor")
    moved_query, moved_key, moved_value = (
        lax.all_to_all(old_query, "section", split_axis=2, concat_axis=0, tiled=True),
        lax.all_to_all(old_key, "section", split_axis=2, concat_axis=0, tiled=True),
        lax.all_to_all(old_value, "section", split_axis=2, concat_axis=0, tiled=True),
    )
    part_query = mix_layers(depth_mix, moved_query)
    part_key = mix_layers(depth_mix, moved_key)
    part_value = mix_layers(depth_mix, moved_value)
    mixed_query, mixed_key, mixed_value = (
        lax.all_gather(part_query, "section", axis=1, tiled=True),
        lax.all_gather(part_key, "section", axis=1, tiled=True),
        lax.all_gather(part_value, "section", axis=1, tiled=True),
    )
    query_width, kv_width = (
        lax.all_gather(width_query, "tensor", axis=1, tiled=True),
        lax.all_gather(width_kv, "tensor", axis=1, tiled=True),
    )
    expanded_query = contract_last(mixed_query, query_width).astype(jnp.bfloat16)
    expanded_key = contract_last(mixed_key, kv_width).astype(jnp.bfloat16)
    expanded_value = contract_last(mixed_value, kv_width).astype(jnp.bfloat16)
    whole_query, whole_key, whole_value = (
        lax.all_gather(expanded_query, "tensor", axis=0, tiled=True),
        lax.all_gather(expanded_key, "tensor", axis=0, tiled=True),
        lax.all_gather(expanded_value, "tensor", axis=0, tiled=True),
    )
    fragment = lax.all_gather(width_stream, "section", axis=1, tiled=True)

    def product_of(whole):
        return jnp.dot(fragment, whole, preferred_element_type=jnp.float32)

    sum_query = product_of(whole_query)
    sum_key = product_of(whole_key)
    sum_value = product_of(whole_value)
    grown_query = sum_query.astype(jnp.bfloat16)
    grown_key = sum_key.astype(jnp.bfloat16)
    grown_value = sum_value.astype(jnp.bfloat16)
    all_hidden = lax.all_gather(hidden, "section", axis=0, tiled=True)
    token_count = all_hidden.shape[0]
    block_rows = token_count // tensor_count
    query_cols = grown_query.shape[1]
    heads_here = query_cols // HD
    head_ids = section_index * heads_here + jnp.arange(heads_here, dtype=jnp.int32)
    kv_ids = head_ids % KVH
    joined = jnp.concatenate([grown_query, grown_key, grown_value], axis=1)
    summed = lax.psum_scatter(
        jnp.dot(all_hidden, joined, preferred_element_type=jnp.float32),
        "tensor",
        scatter_dimension=0,
        tiled=True,
    )
    kv_cols = (summed.shape[1] - query_cols) // 2
    queries = summed[:, :query_cols].astype(jnp.bfloat16)
    key_part = summed[:, query_cols : query_cols + kv_cols].astype(jnp.bfloat16)
    value_part = summed[:, query_cols + kv_cols :].astype(jnp.bfloat16)
    key_wide, value_wide = (
        lax.all_gather(key_part, "section", axis=1, tiled=True),
        lax.all_gather(value_part, "section", axis=1, tiled=True),
    )
    key_here = pick_heads(key_wide, kv_ids)
    value_here = pick_heads(value_wide, kv_ids)
    key_rows, value_rows = (
        lax.all_gather(key_here, "tensor", axis=0, tiled=True),
        lax.all_gather(value_here, "tensor", axis=0, tiled=True),
    )
    query_heads = queries.reshape(block_rows, heads_here, HD)
    key_heads = key_rows.reshape(token_count, heads_here, HD)
    value_heads = value_rows.reshape(token_count, heads_here, HD)
    scores = jnp.einsum(
        "qhd,khd->hqk", query_heads, key_heads, preferred_element_type=jnp.float32
    ) * (1.0 / math.sqrt(HD))
    query_position = tensor_index * block_rows + lax.broadcasted_iota(jnp.int32, (block_rows, 1), 0)
    key_position = lax.broadcasted_iota(jnp.int32, (1, token_count), 1)
    scores = jnp.where((key_position <= query_position)[None], scores, -jnp.inf)
    row_max = jnp.max(scores, axis=2, keepdims=True)
    weights = jnp.exp(scores - row_max)
    denominator = jnp.sum(weights, axis=2, keepdims=True)
    probs = weights.astype(jnp.bfloat16)
    mixed_out = (
        jnp.einsum("hqk,khd->hqd", probs, value_heads, preferred_element_type=jnp.float32)
        / denominator
    )
    attended = (
        jnp.transpose(mixed_out, (1, 0, 2))
        .reshape(block_rows, heads_here * HD)
        .astype(jnp.bfloat16)
    )
    return (grown_query, grown_key, grown_value, attended)


def fits(mesh):
    sections, tensors = mesh.shape["section"], mesh.shape["tensor"]
    return sections == KVH and tensors == 4


def solution(mesh):
    placed = (
        P("section", "tensor", None),
        P("section", "tensor", None),
        P("section", "tensor", None),
        P(),
        P("section", "tensor"),
        P("section", "tensor"),
        P("tensor", "section"),
        P("section", "tensor"),
    )
    return jax.shard_map(
        fast_device if fits(mesh) else plain_device,
        mesh=mesh,
        in_specs=placed,
        out_specs=(
            P("tensor", "section"),
            P("tensor", "section"),
            P("tensor", "section"),
            P("tensor", "section"),
        ),
        check_vma=False,
    )
```

```python
import functools
import math

import jax
import jax.numpy as jnp
from jax import lax
from jax.experimental import pallas as pl
from jax.experimental.pallas import tpu as pltpu
from jax.sharding import PartitionSpec as P

HD = 128
KVH = 8
MIB = 1024 * 1024
ANY = pl.BlockSpec(memory_space=pl.ANY)


def contract_last(left_side, right_side):
    return lax.dot_general(
        left_side, right_side, (((1,), (1,)), ((), ())), preferred_element_type=jnp.float32
    )


def remote(src, dst, send, recv, axis, index):
    return pltpu.make_async_remote_copy(
        src_ref=src,
        dst_ref=dst,
        send_sem=send,
        recv_sem=recv,
        device_id={axis: index},
        device_id_type=pl.DeviceIdType.MESH,
    )


class Place:
    def __init__(self, sections):
        self.count = sections // 2
        self.section = lax.axis_index("section")
        self.tensor = lax.axis_index("tensor")
        self.z = self.section // 2
        self.x = self.section % 2
        self.y = self.tensor // 2
        self.core = self.tensor % 2
        self.other_x = self.z * 2 + 1 - self.x
        self.other_y = (1 - self.y) * 2 + self.core
        self.other_core = self.y * 2 + 1 - self.core


class SectionGather:
    def __init__(self, place, own, view, sems, local_sem=None, on_block=None, wide=False):
        self.p = place
        self.own = view(place.section) if own is None else own
        self.view = view
        self.sems = sems
        self.local = None
        if local_sem is not None:
            self.local = pltpu.make_async_copy(self.own, view(place.section), local_sem)
        self.on_block = on_block
        self.wide = wide

    def copy(self, kind, origin, src):
        p = self.p
        target = (p.section + 2, p.section - 2, p.other_x)[kind - 1]
        return remote(
            src,
            self.view(origin),
            self.sems.at[kind, origin],
            self.sems.at[0, origin],
            "section",
            target,
        )

    def start_z(self):
        p = self.p

        @pl.when(p.z < p.count - 1)
        def _():
            self.copy(1, p.section, self.own).start()

        @pl.when(p.z > 0)
        def _():
            self.copy(2, p.section, self.own).start()

        if self.local is not None:
            self.local.start()

    def start_x(self):
        self.copy(3, self.p.section, self.own).start()

    def start(self):
        if self.wide:
            self.start_x()
            self.start_z()
        else:
            self.start_z()
            self.start_x()

    def arrived(self, origin):
        self.copy(3, origin, self.view(origin)).wait_recv()

    def cross(self):
        p = self.p
        if self.wide:
            origin = p.other_x
            block = self.view(origin)
            self.arrived(origin)

            @pl.when(p.z < p.count - 1)
            def _():
                self.copy(1, origin, block).start()

            @pl.when(p.z > 0)
            def _():
                self.copy(2, origin, block).start()

    def step(self, hop):
        p = self.p

        def take(origin, kind, more):
            block = self.view(origin)
            self.arrived(origin)

            @pl.when(more)
            def _():
                self.copy(kind, origin, block).start()

            if not self.wide:
                self.copy(3, origin, block).start()
            if self.on_block is not None:
                self.on_block(origin)

        columns = (p.section, p.other_x) if self.wide else (p.section,)

        @pl.when(p.z - hop >= 0)
        def _():
            for column in columns:
                take(column - 2 * hop, 1, p.z < p.count - 1)

        @pl.when(p.z + hop < p.count)
        def _():
            for column in columns:
                take(column + 2 * hop, 2, p.z > 0)

    def finish(self):
        p = self.p
        if self.local is not None:
            self.local.wait()
        if not self.wide:
            for other_z in range(p.count):
                across = other_z * 2 + 1 - p.x
                self.arrived(across)
                if self.on_block is not None:
                    self.on_block(across)
        for other_z in range(p.count):
            for column in (p.x, 1 - p.x) if self.wide else (p.x,):
                origin = other_z * 2 + column
                block = self.view(origin)

                @pl.when((other_z <= p.z) & (p.z < p.count - 1))
                def _():
                    self.copy(1, origin, block).wait_send()

                @pl.when((other_z >= p.z) & (p.z > 0))
                def _():
                    self.copy(2, origin, block).wait_send()

            if not self.wide:
                self.copy(3, origin, block).wait_send()
        if self.wide:
            self.copy(3, p.section, self.own).wait_send()


class TensorGather:
    def __init__(self, place, own, view, sems, local_sem):
        p = place
        mine, far = p.tensor, p.other_y
        self.local = pltpu.make_async_copy(own, view(mine), local_sem)
        self.to_y = remote(own, view(mine), sems.at[0], sems.at[1], "tensor", p.other_y)
        self.to_core = remote(own, view(mine), sems.at[2], sems.at[3], "tensor", p.other_core)
        self.far_to_core = remote(
            view(far), view(far), sems.at[4], sems.at[5], "tensor", p.other_core
        )

    def start(self):
        self.to_y.start()
        self.to_core.start()
        self.local.start()

    def forward(self):
        self.to_y.wait_recv()
        self.far_to_core.start()

    def finish(self):
        self.local.wait()
        self.to_y.wait_send()
        self.to_core.wait()
        self.far_to_core.wait()


PARTS = 2


def mix_kernel(
    sections,
    depth_mix,
    old_query,
    old_key,
    old_value,
    width_query,
    width_kv,
    width_stream,
    mixed_query,
    mixed_key,
    mixed_value,
    query_width,
    kv_width,
    fragment,
    held,
    peer,
    sums,
    up,
    down,
    mine,
    load_sems,
    pair_sems,
    ring_sems,
    mixed_sems,
    stream_sems,
    width_sems,
    local_sems,
):
    p = Place(sections)
    count = p.count
    rows = held.shape[1]
    part_rows = rows // PARTS
    q_cols = old_query.shape[1] // sections
    k_cols = old_key.shape[1] // sections
    fields = (
        (old_query, 0, q_cols),
        (old_key, q_cols, k_cols),
        (old_value, q_cols + k_cols, k_cols),
    )
    factor = depth_mix[p.section]
    peer_factor = depth_mix[p.other_x]

    def pair_copies(far):
        for i, (ref, first, width) in enumerate(fields):
            start = pl.multiple_of((far * 2 + 1 - p.x) * width, 128)
            yield remote(
                ref.at[:, pl.ds(start, width)],
                peer.at[far, :, pl.ds(first, width)],
                pair_sems.at[0, far, i],
                pair_sems.at[1, far, i],
                "section",
                p.other_x,
            )

    def at_distance(distance, act):
        @pl.when(p.z + distance < count)
        def _():
            act(p.z + distance)

        if distance:

            @pl.when(p.z - distance >= 0)
            def _():
                act(p.z - distance)

    def send_pair(far):
        for one in pair_copies(far):
            one.start()

    def pair_arrived(far):
        for one in pair_copies(far):
            one.wait_recv()

    at_distance(count - 1, send_pair)

    loads = []
    for far in range(count):
        for i, (ref, first, width) in enumerate(fields):
            start = pl.multiple_of((far * 2 + p.x) * width, 128)
            load = pltpu.make_async_copy(
                ref.at[:, pl.ds(start, width)],
                held.at[far, :, pl.ds(first, width)],
                load_sems.at[3 * far + i],
            )
            load.start()
            loads.append(load)

    stream_rows, stream_cols = width_stream.shape
    wide_rows = stream_rows // 4

    def stream_gather(index, window, wide):
        return SectionGather(
            p,
            width_stream.at[window],
            lambda s: fragment.at[
                window, pl.ds(pl.multiple_of(s * stream_cols, 128), stream_cols)
            ],
            stream_sems.at[index],
            local_sems.at[index],
            wide=wide,
        )

    wide_stream = stream_gather(0, pl.ds(0, wide_rows), True)
    stream = stream_gather(1, pl.ds(wide_rows, stream_rows - wide_rows), False)
    wide_cols, kv_width_cols = width_query.shape[1], width_kv.shape[1]
    widths = [
        TensorGather(
            p,
            width_query,
            lambda t: query_width.at[:, pl.ds(pl.multiple_of(t * wide_cols, 128), wide_cols)],
            width_sems.at[0],
            local_sems.at[2],
        ),
        TensorGather(
            p,
            width_kv,
            lambda t: kv_width.at[
                :, pl.ds(pl.multiple_of(t * kv_width_cols, 128), kv_width_cols)
            ],
            width_sems.at[1],
            local_sems.at[3],
        ),
    ]
    for one in widths:
        one.start()
    wide_stream.start()
    stream.start_z()

    @pl.when(p.z == 0)
    def _():
        up[...] = jnp.zeros(up.shape, up.dtype)

    @pl.when(p.z == count - 1)
    def _():
        down[...] = jnp.zeros(down.shape, down.dtype)

    for load in loads:
        load.wait()

    step_rows = 32

    def ring(direction, distance, part):
        window = pl.ds(part * part_rows, part_rows)
        target = p.section + 2 if direction == 0 else p.section - 2
        slot = p.z + distance - 1 if direction == 0 else p.z - distance
        return remote(
            sums.at[slot, window],
            (up, down)[direction].at[distance - 1, window],
            ring_sems.at[direction, 0, distance - 1, part],
            ring_sems.at[direction, 1, distance - 1, part],
            "section",
            target,
        )

    def ring_arrived(direction, distance, part):
        slot = (up, down)[direction].at[distance - 1, pl.ds(part * part_rows, part_rows)]
        remote(
            slot,
            slot,
            ring_sems.at[direction, 0, distance - 1, part],
            ring_sems.at[direction, 1, distance - 1, part],
            "section",
            p.other_x,
        ).wait_recv()

    def pair_sum(far, window):
        value = held[far, window, :].astype(jnp.float32) * factor
        return value + peer[far, window, :].astype(jnp.float32) * peer_factor

    def relay(direction, distance, part):
        slots = (up, down)[direction]
        far = p.z + distance if direction == 0 else p.z - distance
        slot = p.z + distance - 1 if direction == 0 else p.z - distance
        sends = far < count if direction == 0 else far >= 0
        receives = p.z > 0 if direction == 0 else p.z < count - 1

        @pl.when(sends)
        def _():
            if distance < count - 1:

                @pl.when(receives)
                def _():
                    ring_arrived(direction, distance + 1, part)

            @pl.loop(0, part_rows // step_rows)
            def _(i):
                window = pl.ds(
                    pl.multiple_of(part * part_rows + i * step_rows, step_rows), step_rows
                )
                value = pair_sum(far, window)
                if distance < count - 1:
                    value += slots[distance, window, :]
                sums[slot, window, :] = value

            if distance < count - 1:
                beyond = far + 1 < count if direction == 0 else far - 1 >= 0

                @pl.when(beyond)
                def _():
                    ring(direction, distance + 1, part).wait_send()

            ring(direction, distance, part).start()

    for distance in range(count - 1, 0, -1):
        at_distance(distance, pair_arrived)
        at_distance(distance - 1, send_pair)
        if distance == 1:
            stream.start_x()
        for part in range(PARTS):
            relay(0, distance, part)
            relay(1, distance, part)
        if distance == count - 1:
            wide_stream.cross()
        if distance == min(2, count - 1):
            for one in widths:
                one.forward()
            wide_stream.step(1)
            stream.step(1)
    for hop in range(2, count - 1):
        wide_stream.step(hop)
        stream.step(hop)
    at_distance(0, pair_arrived)

    gathers = []
    for part in range(PARTS):

        @pl.when(p.z > 0)
        def _():
            ring_arrived(0, 1, part)

        @pl.when(p.z < count - 1)
        def _():
            ring_arrived(1, 1, part)

        @pl.loop(0, part_rows // step_rows)
        def _(i):
            window = pl.ds(pl.multiple_of(part * part_rows + i * step_rows, step_rows), step_rows)
            value = pair_sum(p.z, window) + up[0, window, :] + down[0, window, :]
            mine[window, :] = value.astype(jnp.bfloat16)

        window = pl.ds(part * part_rows, part_rows)
        for i, (ref, first, width) in enumerate(
            (
                (mixed_query, 0, q_cols),
                (mixed_key, q_cols, k_cols),
                (mixed_value, q_cols + k_cols, k_cols),
            )
        ):
            gather = SectionGather(
                p,
                mine.at[window, pl.ds(first, width)],
                lambda s, ref=ref, width=width, window=window: ref.at[
                    window, pl.ds(pl.multiple_of(s * width, 128), width)
                ],
                mixed_sems.at[3 * part + i],
                local_sems.at[4 + 3 * part + i],
                wide=i == 0 and part == 0,
            )
            gather.start()
            gathers.append(gather)
    if count > 2:
        wide_stream.step(count - 1)
        stream.step(count - 1)
    for gather in gathers:
        gather.cross()
    for hop in range(1, count):
        for gather in gathers:
            gather.step(hop)

    for far in range(count):
        for one in pair_copies(far):
            one.wait_send()
    for part in range(PARTS):

        @pl.when(p.z < count - 1)
        def _():
            ring(0, 1, part).wait_send()

        @pl.when(p.z > 0)
        def _():
            ring(1, 1, part).wait_send()

    wide_stream.finish()
    stream.finish()
    for one in widths:
        one.finish()
    for gather in gathers:
        gather.finish()


def spread_kernel(
    sections,
    expanded,
    hidden,
    whole,
    all_hidden,
    expanded_sems,
    hidden_sems,
    local_sems,
):
    p = Place(sections)
    rows, tokens = expanded.shape[0], hidden.shape[0]
    wide = TensorGather(
        p,
        expanded,
        lambda t: whole.at[pl.ds(pl.multiple_of(t * rows, 16), rows)],
        expanded_sems,
        local_sems.at[0],
    )
    wide_tokens = tokens // 8
    half = (tokens - wide_tokens) // 2
    states = [
        SectionGather(
            p,
            hidden.at[pl.ds(first, size)],
            lambda s, first=first, size=size: all_hidden.at[
                pl.ds(pl.multiple_of(s * tokens + first, 16), size)
            ],
            hidden_sems.at[index],
            local_sems.at[1 + index],
            wide=index == 0,
        )
        for index, (first, size) in enumerate(
            ((0, wide_tokens), (wide_tokens, half), (wide_tokens + half, half))
        )
    ]
    wide.start()
    for one in states:
        one.start()
    for one in states:
        one.cross()
    for hop in range(1, p.count):
        for one in states:
            one.step(hop)
    wide.forward()
    for one in states:
        one.finish()
    wide.finish()


def sum_kernel(
    sections,
    partial,
    queries,
    joint,
    near,
    from_core,
    y_out,
    y_in,
    own,
    near_sems,
    core_sems,
    y_sems,
    own_y_sems,
    joint_sems,
    local_sems,
    side_sems,
):
    p = Place(sections)
    rows = near.shape[1]
    q_cols = queries.shape[1]
    joint_cols = own.shape[1]
    spans = ((q_cols, joint_cols), (0, q_cols))

    def core_copy(span, row_y):
        first, width = spans[span]
        block = row_y * 2 + 1 - p.core
        return remote(
            partial.at[pl.ds(pl.multiple_of(block * rows, 16), rows), pl.ds(first, width)],
            from_core.at[row_y, :, pl.ds(first, width)],
            core_sems.at[0, span, row_y],
            core_sems.at[1, span, row_y],
            "tensor",
            p.other_core,
        )

    def near_copy(span, row_y):
        first, width = spans[span]
        block = row_y * 2 + p.core
        return pltpu.make_async_copy(
            partial.at[pl.ds(pl.multiple_of(block * rows, 16), rows), pl.ds(first, width)],
            near.at[row_y, :, pl.ds(first, width)],
            near_sems.at[span, row_y],
        )

    def y_copy(span):
        first, width = spans[span]
        return remote(
            y_out.at[:, pl.ds(first, width)],
            y_in.at[:, pl.ds(first, width)],
            y_sems.at[0, span],
            y_sems.at[1, span],
            "tensor",
            p.other_y,
        )

    step_rows = 32

    def each_window(body):
        @pl.loop(0, rows // step_rows)
        def _(i):
            body(pl.ds(pl.multiple_of(i * step_rows, step_rows), step_rows))

    def core_sum(span, row_y, window):
        first, width = spans[span]
        columns = pl.ds(first, width)
        return near[row_y, window, columns] + from_core[row_y, window, columns]

    def send_sum(span):
        first, width = spans[span]
        near_copy(span, 1 - p.y).wait()
        core_copy(span, 1 - p.y).wait_recv()

        def body(window):
            y_out[window, pl.ds(first, width)] = core_sum(span, 1 - p.y, window).astype(
                jnp.bfloat16
            )

        each_window(body)
        y_copy(span).start()

    def take_sum(span, target):
        first, width = spans[span]
        near_copy(span, p.y).wait()
        core_copy(span, p.y).wait_recv()
        y_copy(span).wait_recv()

        def body(window):
            value = core_sum(span, p.y, window)
            value += y_in[window, pl.ds(first, width)].astype(jnp.float32)
            target[window, :] = value.astype(jnp.bfloat16)

        each_window(body)

    for span in range(2):
        for row_y in (1 - p.y, p.y):
            core_copy(span, row_y).start()
            near_copy(span, row_y).start()

    def block(t, s):
        return joint.at[
            pl.ds(pl.multiple_of(t * rows, 16), rows),
            pl.ds(pl.multiple_of(s * joint_cols, 128), joint_cols),
        ]

    def side(row_y, core, s, src):
        return remote(
            src,
            block(row_y * 2 + core, s),
            side_sems.at[row_y, 0, s],
            side_sems.at[row_y, 1, s],
            "tensor",
            p.other_core,
        )

    def hand_on(row_y):
        def act(s):
            side(row_y, p.core, s, block(row_y * 2 + p.core, s)).start()

        return act

    send_sum(0)
    take_sum(0, own)
    own_y = remote(
        own,
        block(p.tensor, p.section),
        own_y_sems.at[0],
        own_y_sems.at[1],
        "tensor",
        p.other_y,
    )
    own_y.start()
    near_gather = SectionGather(
        p, own, lambda s: block(p.tensor, s), joint_sems.at[0], local_sems.at[0], hand_on(p.y)
    )
    far_gather = SectionGather(
        p, None, lambda s: block(p.other_y, s), joint_sems.at[1], None, hand_on(1 - p.y)
    )
    near_gather.start()
    side(p.y, p.core, p.section, own).start()
    own_y.wait_recv()
    far_gather.start()
    side(1 - p.y, p.core, p.section, block(p.other_y, p.section)).start()
    send_sum(1)
    for hop in range(1, p.count):
        near_gather.step(hop)
        far_gather.step(hop)
    take_sum(1, queries)
    near_gather.finish()
    far_gather.finish()

    @pl.loop(0, sections)
    def _(s):
        for row_y in range(2):
            from_other = block(row_y * 2 + 1 - p.core, s)
            side(row_y, 1 - p.core, s, from_other).wait_recv()
            side(row_y, p.core, s, block(row_y * 2 + p.core, s)).wait_send()

    own_y.wait_send()
    for span in range(2):
        y_copy(span).wait_send()
        for row_y in (1 - p.y, p.y):
            core_copy(span, row_y).wait_send()


GROUP = 2


def attend_kernel(first, queries, joint, attended):
    rows = queries.shape[0]
    tensor_index = first[0]
    scale = 1.0 / math.sqrt(HD) / math.log(2.0)

    def span(index):
        return pl.ds(pl.multiple_of(index * rows, 128), rows)

    def scores_of(index, i):
        keys = joint[span(index), 2 * i * HD : (2 * i + 1) * HD]
        return contract_last(queries[:, i * HD : (i + 1) * HD], keys)

    def values_of(index, i):
        return joint[span(index), (2 * i + 1) * HD : (2 * i + 2) * HD]

    def opening(i):
        scores = scores_of(tensor_index, i)
        row_of = lax.broadcasted_iota(jnp.int32, (rows, rows), 0)
        column_of = lax.broadcasted_iota(jnp.int32, (rows, rows), 1)
        scores = jnp.where(column_of <= row_of, scores, -jnp.inf)
        top = jnp.max(scores, axis=1, keepdims=True)
        weights = jnp.exp2((scores - top) * scale)
        bottom = jnp.sum(weights, axis=1, keepdims=True)
        running = jnp.dot(
            weights.astype(jnp.bfloat16),
            values_of(tensor_index, i),
            preferred_element_type=jnp.float32,
        )
        return top, bottom, running

    def merge(index, i, carry):
        top, bottom, running = carry
        scores = scores_of(index, i)
        best = jnp.maximum(top, jnp.max(scores, axis=1, keepdims=True))
        weights = jnp.exp2((scores - best) * scale)
        shrink = jnp.exp2((top - best) * scale)
        bottom = bottom * shrink + jnp.sum(weights, axis=1, keepdims=True)
        running = running * shrink + jnp.dot(
            weights.astype(jnp.bfloat16), values_of(index, i), preferred_element_type=jnp.float32
        )
        return best, bottom, running

    state = lax.fori_loop(
        0,
        tensor_index,
        lambda index, state: tuple(merge(index, i, one) for i, one in enumerate(state)),
        tuple(opening(i) for i in range(GROUP)),
    )
    for i, (_, bottom, running) in enumerate(state):
        attended[:, i * HD : (i + 1) * HD] = (running / bottom).astype(jnp.bfloat16)


def attend(queries, joint, tensor_index):
    rows, cols = queries.shape
    tokens = joint.shape[0]
    return pl.pallas_call(
        attend_kernel,
        out_shape=jax.ShapeDtypeStruct((rows, cols), jnp.bfloat16),
        grid_spec=pltpu.PrefetchScalarGridSpec(
            num_scalar_prefetch=1,
            grid=(cols // (GROUP * HD),),
            in_specs=[
                pl.BlockSpec((rows, GROUP * HD), lambda h, first: (0, h)),
                pl.BlockSpec((tokens, 2 * GROUP * HD), lambda h, first: (0, h % (KVH // GROUP))),
            ],
            out_specs=pl.BlockSpec((rows, GROUP * HD), lambda h, first: (0, h)),
        ),
        compiler_params=pltpu.CompilerParams(vmem_limit_bytes=58 * MIB),
    )(tensor_index.reshape(1).astype(jnp.int32), queries, joint)


def fast_device(
    old_query, old_key, old_value, depth_mix, width_query, width_kv, width_stream, hidden
):
    sections = lax.axis_size("section")
    tensors = lax.axis_size("tensor")
    count = sections // 2
    bf16 = jnp.bfloat16
    dma = pltpu.SemaphoreType.DMA
    rows, model_cols = old_query.shape[1:]
    kv_cols = old_key.shape[2]
    seg = (model_cols + 2 * kv_cols) // sections
    stream_rows, stream_cols = width_stream.shape
    head_cols = width_query.shape[0]
    kv_head_cols = width_kv.shape[0]

    mixed_query, mixed_key, mixed_value, query_width, kv_width, fragment = pl.pallas_call(
        functools.partial(mix_kernel, sections),
        out_shape=[
            jax.ShapeDtypeStruct((rows, model_cols), bf16),
            jax.ShapeDtypeStruct((rows, kv_cols), bf16),
            jax.ShapeDtypeStruct((rows, kv_cols), bf16),
            jax.ShapeDtypeStruct((head_cols, model_cols), bf16),
            jax.ShapeDtypeStruct((kv_head_cols, kv_cols), bf16),
            jax.ShapeDtypeStruct((stream_rows, stream_cols * sections), bf16),
        ],
        in_specs=[pl.BlockSpec(memory_space=pltpu.SMEM)] + [ANY] * 6,
        out_specs=[ANY] * 6,
        scratch_shapes=[
            pltpu.VMEM((count, rows, seg), bf16),
            pltpu.VMEM((count, rows, seg), bf16),
            pltpu.VMEM((count - 1, rows, seg), jnp.float32),
            pltpu.VMEM((count - 1, rows, seg), jnp.float32),
            pltpu.VMEM((count - 1, rows, seg), jnp.float32),
            pltpu.VMEM((rows, seg), bf16),
            dma((3 * count,)),
            dma((2, count, 3)),
            dma((2, 2, count - 1, PARTS)),
            dma((3 * PARTS, 4, sections)),
            dma((2, 4, sections)),
            dma((2, 6)),
            dma((4 + 3 * PARTS,)),
        ],
        compiler_params=pltpu.CompilerParams(
            vmem_limit_bytes=52 * MIB, has_side_effects=True
        ),
    )(depth_mix, old_query[0], old_key[0], old_value[0], width_query, width_kv, width_stream)

    expanded = jnp.concatenate(
        [
            contract_last(mixed_query, query_width).astype(bf16),
            contract_last(mixed_key, kv_width).astype(bf16),
            contract_last(mixed_value, kv_width).astype(bf16),
        ],
        axis=1,
    )
    joined_cols = expanded.shape[1]
    token_part, feature_cols = hidden.shape
    tokens = token_part * sections

    whole, all_hidden = pl.pallas_call(
        functools.partial(spread_kernel, sections),
        out_shape=[
            jax.ShapeDtypeStruct((rows * tensors, joined_cols), bf16),
            jax.ShapeDtypeStruct((tokens, feature_cols), bf16),
        ],
        in_specs=[ANY] * 2,
        out_specs=[ANY] * 2,
        scratch_shapes=[dma((6,)), dma((3, 4, sections)), dma((4,))],
        compiler_params=pltpu.CompilerParams(
            vmem_limit_bytes=16 * MIB, has_side_effects=True
        ),
    )(expanded, hidden)

    grown = jnp.dot(fragment, whole, preferred_element_type=jnp.float32).astype(bf16)
    partial = jnp.dot(all_hidden, grown, preferred_element_type=jnp.float32)
    block_rows = tokens // tensors
    queries, joint = pl.pallas_call(
        functools.partial(sum_kernel, sections),
        out_shape=[
            jax.ShapeDtypeStruct((block_rows, head_cols), bf16),
            jax.ShapeDtypeStruct((tokens, 2 * kv_head_cols * sections), bf16),
        ],
        in_specs=[ANY],
        out_specs=[pl.BlockSpec(memory_space=pltpu.VMEM), ANY],
        scratch_shapes=[
            pltpu.VMEM((2, block_rows, joined_cols), jnp.float32),
            pltpu.VMEM((2, block_rows, joined_cols), jnp.float32),
            pltpu.VMEM((block_rows, joined_cols), bf16),
            pltpu.VMEM((block_rows, joined_cols), bf16),
            pltpu.VMEM((block_rows, 2 * kv_head_cols), bf16),
            dma((2, 2)),
            dma((2, 2, 2)),
            dma((2, 2)),
            dma((2,)),
            dma((2, 4, sections)),
            dma((1,)),
            dma((2, 2, sections)),
        ],
        compiler_params=pltpu.CompilerParams(
            vmem_limit_bytes=56 * MIB, has_side_effects=True
        ),
    )(partial)

    attended = attend(queries, joint, lax.axis_index("tensor"))
    return (
        grown[:, :head_cols],
        grown[:, head_cols : head_cols + kv_head_cols],
        grown[:, head_cols + kv_head_cols :],
        attended,
    )


def mix_layers(depth_mix, stacked):
    flattened = stacked.reshape(stacked.shape[0], -1)
    mixed = jnp.dot(
        depth_mix, flattened, precision=lax.Precision.HIGHEST, preferred_element_type=jnp.float32
    )
    return mixed.reshape(stacked.shape[1:]).astype(jnp.bfloat16)


def pick_heads(wide, kv_ids):
    row_count = wide.shape[0]
    grouped = wide.reshape(row_count, KVH, HD)
    chosen = jnp.take(grouped, kv_ids, axis=1)
    return chosen.reshape(row_count, kv_ids.shape[0] * HD)


def plain_device(
    old_query, old_key, old_value, depth_mix, width_query, width_kv, width_stream, hidden
):
    section_index = lax.axis_index("section")
    tensor_index = lax.axis_index("tensor")
    tensor_count = lax.axis_size("tensor")
    moved_query, moved_key, moved_value = (
        lax.all_to_all(old_query, "section", split_axis=2, concat_axis=0, tiled=True),
        lax.all_to_all(old_key, "section", split_axis=2, concat_axis=0, tiled=True),
        lax.all_to_all(old_value, "section", split_axis=2, concat_axis=0, tiled=True),
    )
    part_query = mix_layers(depth_mix, moved_query)
    part_key = mix_layers(depth_mix, moved_key)
    part_value = mix_layers(depth_mix, moved_value)
    mixed_query, mixed_key, mixed_value = (
        lax.all_gather(part_query, "section", axis=1, tiled=True),
        lax.all_gather(part_key, "section", axis=1, tiled=True),
        lax.all_gather(part_value, "section", axis=1, tiled=True),
    )
    query_width, kv_width = (
        lax.all_gather(width_query, "tensor", axis=1, tiled=True),
        lax.all_gather(width_kv, "tensor", axis=1, tiled=True),
    )
    expanded_query = contract_last(mixed_query, query_width).astype(jnp.bfloat16)
    expanded_key = contract_last(mixed_key, kv_width).astype(jnp.bfloat16)
    expanded_value = contract_last(mixed_value, kv_width).astype(jnp.bfloat16)
    whole_query, whole_key, whole_value = (
        lax.all_gather(expanded_query, "tensor", axis=0, tiled=True),
        lax.all_gather(expanded_key, "tensor", axis=0, tiled=True),
        lax.all_gather(expanded_value, "tensor", axis=0, tiled=True),
    )
    fragment = lax.all_gather(width_stream, "section", axis=1, tiled=True)

    def product_of(whole):
        return jnp.dot(fragment, whole, preferred_element_type=jnp.float32)

    sum_query = product_of(whole_query)
    sum_key = product_of(whole_key)
    sum_value = product_of(whole_value)
    grown_query = sum_query.astype(jnp.bfloat16)
    grown_key = sum_key.astype(jnp.bfloat16)
    grown_value = sum_value.astype(jnp.bfloat16)
    all_hidden = lax.all_gather(hidden, "section", axis=0, tiled=True)
    token_count = all_hidden.shape[0]
    block_rows = token_count // tensor_count
    query_cols = grown_query.shape[1]
    heads_here = query_cols // HD
    head_ids = section_index * heads_here + jnp.arange(heads_here, dtype=jnp.int32)
    kv_ids = head_ids % KVH
    joined = jnp.concatenate([grown_query, grown_key, grown_value], axis=1)
    summed = lax.psum_scatter(
        jnp.dot(all_hidden, joined, preferred_element_type=jnp.float32),
        "tensor",
        scatter_dimension=0,
        tiled=True,
    )
    kv_cols = (summed.shape[1] - query_cols) // 2
    queries = summed[:, :query_cols].astype(jnp.bfloat16)
    key_part = summed[:, query_cols : query_cols + kv_cols].astype(jnp.bfloat16)
    value_part = summed[:, query_cols + kv_cols :].astype(jnp.bfloat16)
    key_wide, value_wide = (
        lax.all_gather(key_part, "section", axis=1, tiled=True),
        lax.all_gather(value_part, "section", axis=1, tiled=True),
    )
    key_here = pick_heads(key_wide, kv_ids)
    value_here = pick_heads(value_wide, kv_ids)
    key_rows, value_rows = (
        lax.all_gather(key_here, "tensor", axis=0, tiled=True),
        lax.all_gather(value_here, "tensor", axis=0, tiled=True),
    )
    query_heads = queries.reshape(block_rows, heads_here, HD)
    key_heads = key_rows.reshape(token_count, heads_here, HD)
    value_heads = value_rows.reshape(token_count, heads_here, HD)
    scores = jnp.einsum(
        "qhd,khd->hqk", query_heads, key_heads, preferred_element_type=jnp.float32
    ) * (1.0 / math.sqrt(HD))
    query_position = tensor_index * block_rows + lax.broadcasted_iota(jnp.int32, (block_rows, 1), 0)
    key_position = lax.broadcasted_iota(jnp.int32, (1, token_count), 1)
    scores = jnp.where((key_position <= query_position)[None], scores, -jnp.inf)
    row_max = jnp.max(scores, axis=2, keepdims=True)
    weights = jnp.exp(scores - row_max)
    denominator = jnp.sum(weights, axis=2, keepdims=True)
    probs = weights.astype(jnp.bfloat16)
    mixed_out = (
        jnp.einsum("hqk,khd->hqd", probs, value_heads, preferred_element_type=jnp.float32)
        / denominator
    )
    attended = (
        jnp.transpose(mixed_out, (1, 0, 2))
        .reshape(block_rows, heads_here * HD)
        .astype(jnp.bfloat16)
    )
    return (grown_query, grown_key, grown_value, attended)


def fits(mesh):
    sections, tensors = mesh.shape["section"], mesh.shape["tensor"]
    return sections == KVH and tensors == 4


def solution(mesh):
    placed = (
        P("section", "tensor", None),
        P("section", "tensor", None),
        P("section", "tensor", None),
        P(),
        P("section", "tensor"),
        P("section", "tensor"),
        P("tensor", "section"),
        P("section", "tensor"),
    )
    return jax.shard_map(
        fast_device if fits(mesh) else plain_device,
        mesh=mesh,
        in_specs=placed,
        out_specs=(
            P("tensor", "section"),
            P("tensor", "section"),
            P("tensor", "section"),
            P("tensor", "section"),
        ),
        check_vma=False,
    )
```
